512 devices in a mesh: user: 32 (over x, z), seq: 16 (over y, core).
Axes of the slice: x: 4, y: 8, z: 8, core: 2. Of those that a mesh axis runs over, the one named last changes fastest.
Arguments:
- hist_feat: bfloat16 [32, 2048, 1024], P('user', 'seq'), may hold values from -6 to 6
- hist_length: int32 [32], P('user'), may hold values from 512 to 2048, as said below
- time_bucket: int32 [32, 2048], P('user', 'seq'), may hold values from 0 to 31
- cand_feat: bfloat16 [16384, 1024], P(('user', 'seq')), may hold values from -6 to 6
- cand_owner: int32 [16384, 1], P(('user', 'seq')), may hold values from 0 to 31; in each aligned block of 32 rows (0 to 31, 32 to 63, ...) at most 2 rows name the same one
- proj_weight: bfloat16 [1024, 16, 256], P(None, 'seq'), may hold values from -0.1875 to 0.1875
- time_bias: float32 [16, 32], replicated, may hold values from -4 to 4
- norm_gain: float32 [1024], replicated, may hold values from 0.1 to 1.9
- out_weight: bfloat16 [1024, 1024], replicated, may hold values from -0.1875 to 0.1875
Outputs:
- hist_out: bfloat16 [32, 2048, 1024], P('user', 'seq')
- cand_out: bfloat16 [16384, 1024], P(('user', 'seq'))
The draws below stay inside these ranges and needn't reach their ends.
Inputs may be any that keep to these rules, and one draw needn't show every extreme that they name: `hist_length`: some user's history has exactly 2048 valid events; events at or beyond a user's length are padding. `cand_owner`: the 32 candidate rows of one device name one user at most 2 times, and some device names some user exactly 2 times.
All inputs are finite; a program needn't handle non-finite values.
Results may differ from the reference program's by a relative error of at most 0.0058.
Values may be sent and summed in bfloat16 or wider, within the bound.
A program may use at most 64 MiB of HBM per device.

```python
import math
import jax
import jax.numpy as jnp
import numpy as np
from jax import lax

D = 1024
H = 16
DH = 64
NB = 32
CAND_DEV = 32
CAP = 2
HIST = 2048
USERS = 32
CANDS = 16384
N_USER = 32
N_SEQ = 16


def draw_hist_length(key, part):
    key = jax.random.fold_in(key, 11)
    key_lengths, key_longest = jax.random.split(key)
    lengths = jax.random.randint(key_lengths, (USERS,), HIST // 4, HIST + 1, dtype=jnp.int32)
    longest = jax.random.randint(key_longest, (), 0, USERS, dtype=jnp.int32)
    return jnp.where(jnp.arange(USERS, dtype=jnp.int32) == longest, HIST, lengths).astype(jnp.int32)


def plant(entries, rng, least, largest):
    longest = entries.shape.index(max(entries.shape))
    spots = []
    for shift in (0, 1):
        where = [jax.random.randint(jax.random.fold_in(rng, axis), (), 0, length) for axis, length in enumerate(entries.shape)]
        where[longest] = (where[longest] + shift) % entries.shape[longest]
        spots.append(tuple(where))
    return entries.at[spots[0]].set(least).at[spots[1]].set(largest)


def block_scale(own_key, dims, shards, least, largest):
    def one(axis_at, parts):
        steps = jax.random.uniform(jax.random.fold_in(jax.random.fold_in(own_key, 6), axis_at), (parts,), jnp.float32, least / len(shards), largest / len(shards))
        return jnp.repeat(jnp.exp(steps), dims[axis_at] // parts).reshape((-1,) + (1,) * (len(dims) - axis_at - 1))

    factor_of = one(*shards[0])
    for cut in shards[1:]:
        factor_of = factor_of * one(*cut)
    return factor_of


def deal_out(stream_key, own, number, rows, number_of, top, bound, skew):
    ranking = jax.random.permutation(stream_key, number_of)
    heavy_load, ordinary = load_shares(number_of, rows * top, bound, skew, True), load_shares(number_of, rows * top, bound, skew, False)
    places = jnp.arange(number_of)

    def named(tallies, rotation):
        used = int((tallies > 0).sum())
        fixed = max(1, used // 4)
        shifted = fixed + (places - fixed + rotation * (used - fixed)) % max(1, number_of - fixed)
        return jnp.zeros((number_of,), jnp.int32).at[ranking[jnp.where(places < fixed, places, shifted)]].set(jnp.asarray(tallies, jnp.int32))

    tallies = jnp.where(number % 4 == 0, named(heavy_load, number // 4), named(ordinary, number - number // 4 - 1))
    mixed = jax.random.permutation(jax.random.fold_in(own, 3), number_of)
    donor, receiver = mixed[0:number_of // 2 * 2:2], mixed[1:number_of // 2 * 2:2]
    margin = jnp.minimum(tallies[donor] - 1, bound - tallies[receiver]) // 2
    margin = jnp.where((donor == ranking[0]) | (receiver == ranking[0]) | (tallies[receiver] == 0), 0, jnp.maximum(margin, 0))
    shifted = jax.random.randint(jax.random.fold_in(own, 4), (number_of // 2,), 0, 1 << 20) % (margin + 1)
    tallies = tallies.at[donor].add(-shifted).at[receiver].add(shifted)
    items = jnp.searchsorted(jnp.cumsum(tallies), jnp.arange(rows * top), side="right").astype(jnp.int32)
    listing = items.reshape(top, rows).T
    listing = listing[jax.random.permutation(jax.random.fold_in(own, 1), rows)]
    rotation = jax.random.randint(jax.random.fold_in(own, 2), (rows, 1), 0, top)
    return jnp.take_along_axis(listing, (jnp.arange(top)[None, :] + rotation) % top, axis=1)


def load_shares(amount, total, most, skew, full):
    loads = [(1 << 20) // math.isqrt(grade ** skew) + 1 for grade in range(1, amount + 1)]
    largest = most if full else min(most, max(-(-total // amount), total * loads[0] // sum(loads)))
    least = 1 if total - largest >= amount - 1 else 0
    holding, surplus = [largest] + [least] * (amount - 1), total - largest - least * (amount - 1)
    while surplus > 0:
        movable = [i for i in range(1, amount) if holding[i] < largest] or [i for i in range(1, amount) if holding[i] < most]
        mass, budget = sum([loads[i] for i in movable]), surplus
        for i in movable:
            extra = min(most - holding[i], max(1, budget * loads[i] // mass), surplus)
            holding[i] = holding[i] + extra
            surplus = surplus - extra
    return np.array(holding)


def scatter_about(stream_key, dims, spread, bound, shards=(), kind=jnp.bfloat16):
    values = jax.random.normal(stream_key, dims, jnp.float32) * spread
    if len(shards) > 0:
        values = block_scale(stream_key, dims, shards, -0.22, 0.18) * values
    return jnp.clip(values, min=-bound, max=bound).astype(kind)


def setup_inputs(seed: int = 0) -> dict:
    seeds = jax.random.split(jax.random.key(seed), 10)
    hist_feat = scatter_about(seeds[0], (USERS, HIST, D), 1.0, 6.0, ((0, 32), (1, 16)))
    hist_length = draw_hist_length(jax.random.fold_in(seeds[9], 71), 0)
    time_bucket = plant(jax.random.randint(seeds[2], (USERS, HIST), 0, NB), jax.random.fold_in(seeds[2], 1), 0, NB - 1).astype(jnp.int32)
    cand_feat = scatter_about(seeds[3], (CANDS, D), 1.0, 6.0, ((0, 512),))
    cand_owner_keys = jax.random.split(jax.random.fold_in(seeds[4], 1), CANDS // CAND_DEV)
    cand_owner_turns = jax.random.permutation(jax.random.fold_in(seeds[4], 3), CANDS // CAND_DEV)
    cand_owner = jax.vmap(lambda own, number: deal_out(jax.random.fold_in(seeds[4], 2), own, number, CAND_DEV, USERS, 1, CAP, 2))(cand_owner_keys, cand_owner_turns).reshape((CANDS, 1))
    proj_weight = scatter_about(seeds[5], (D, H, 4 * DH), D ** -0.5, 0.1875, ((1, 16),))
    time_bias = scatter_about(seeds[6], (H, NB), 1.0, 4.0, (), jnp.float32)
    norm_gain = jnp.clip(1.0 + 0.18 * jax.random.normal(seeds[7], (H * DH,), jnp.float32), 0.1, 1.9)
    out_weight = scatter_about(seeds[8], (H * DH, D), (H * DH) ** -0.5, 0.1875)
    return {"hist_feat": hist_feat, "hist_length": hist_length, "time_bucket": time_bucket, "cand_feat": cand_feat, "cand_owner": cand_owner, "proj_weight": proj_weight, "time_bias": time_bias, "norm_gain": norm_gain, "out_weight": out_weight}


norm_eps = 1e-05

def project_rows(row_block, weight):
    projected = jnp.dot(row_block, weight.reshape(weight.shape[0], -1), preferred_element_type=jnp.float32)
    return jax.nn.silu(projected).astype(jnp.bfloat16).reshape(row_block.shape[0], H, 4 * DH)

def finish_rows(attention, gate_vals, inputs, norm_gain, out_weight):
    row_total = inputs.shape[0]
    attn_flat = attention.reshape(row_total, -1).astype(jnp.float32)
    row_mean = lax.optimization_barrier(jnp.mean(attn_flat, axis=1, keepdims=True))
    centred = attn_flat - row_mean
    row_var = lax.optimization_barrier(jnp.mean(centred * centred, axis=1, keepdims=True))
    gated_rows = (centred * lax.rsqrt(row_var + norm_eps) * norm_gain * gate_vals.reshape(row_total, -1).astype(jnp.float32)).astype(jnp.bfloat16)
    result = jnp.dot(gated_rows, out_weight, preferred_element_type=jnp.float32) + inputs.astype(jnp.float32)
    return result.astype(jnp.bfloat16)

def attend_heads(queries, key_rows, value_rows, key_bias, limits, length):
    key_pos = jnp.arange(HIST, dtype=jnp.int32)
    keep_mask = (key_pos[None, :] <= limits[:, None]) & (key_pos[None, :] < length)

    def one_head(operands):
        query_head, key_head, value_head, bias_head = operands
        scores = jnp.dot(query_head, key_head.T, preferred_element_type=jnp.float32) * DH ** (-0.5) + bias_head[None, :]
        weights = jnp.where(keep_mask, jax.nn.silu(scores), 0.0).astype(jnp.bfloat16)
        return jnp.dot(weights, value_head, preferred_element_type=jnp.float32).astype(jnp.bfloat16)
    per_head = lax.map(one_head, (queries.transpose(1, 0, 2), key_rows.transpose(1, 0, 2), value_rows.transpose(1, 0, 2), key_bias))
    return per_head.transpose(1, 0, 2)

def reference(hist_feat, hist_length, time_bucket, cand_feat, cand_owner, proj_weight, time_bias, norm_gain, out_weight):
    sources = N_USER * N_SEQ
    owner_ids = cand_owner[:, 0].reshape(sources, CAND_DEV)
    positions = jnp.arange(CAND_DEV, dtype=jnp.int32)
    earlier = positions[None, :] < positions[:, None]
    same_owner = owner_ids[:, :, None] == owner_ids[:, None, :]
    slot_rank = lax.optimization_barrier(jnp.sum(jnp.where(same_owner & earlier[None], 1, 0), axis=2)).astype(jnp.int32)
    slot_column = (jnp.arange(sources, dtype=jnp.int32)[:, None] * CAP + slot_rank).reshape(-1)
    owner_flat = owner_ids.reshape(-1)
    cand_slots = jnp.zeros((USERS, sources * CAP, D), cand_feat.dtype).at[owner_flat, slot_column].set(cand_feat)
    everything = jnp.full((sources * CAP,), HIST - 1, dtype=jnp.int32)
    causal = jnp.arange(HIST, dtype=jnp.int32)

    def per_user(user_index):
        user_rows = hist_feat[user_index]
        slot_rows = cand_slots[user_index]
        hist_proj = project_rows(user_rows, proj_weight)
        cand_proj = project_rows(slot_rows, proj_weight)
        key_bias = time_bias[:, time_bucket[user_index]]
        length = hist_length[user_index]
        key_rows = hist_proj[:, :, 3 * DH:]
        values = hist_proj[:, :, DH:2 * DH]
        hist_attn = attend_heads(hist_proj[:, :, 2 * DH:3 * DH], key_rows, values, key_bias, causal, length)
        cand_attn = attend_heads(cand_proj[:, :, 2 * DH:3 * DH], key_rows, values, key_bias, everything, length)
        hist_done = finish_rows(hist_attn, hist_proj[:, :, :DH], user_rows, norm_gain, out_weight)
        cand_done = finish_rows(cand_attn, cand_proj[:, :, :DH], slot_rows, norm_gain, out_weight)
        return (hist_done, cand_done)
    hist_out, slot_out = lax.map(per_user, jnp.arange(USERS, dtype=jnp.int32))
    return (hist_out, slot_out[owner_flat, slot_column])
```

```python
import functools

import jax
import jax.numpy as jnp
from jax import lax
from jax.experimental import pallas as pl
from jax.experimental.pallas import tpu as pltpu
from jax.sharding import PartitionSpec as P

MESH = pl.DeviceIdType.MESH
NORM_EPS = 1e-05
NX, NZ, NY = 4, 8, 8
NU, NS = NX * NZ, NY * 2
D = 1024
DH = 64
NB = 32
HR = 128
CR = 64
HIST = HR * NS
PAY_V = 2 * HR
PAY_Q = 3 * HR
PAY_B = 3 * HR + CR
PAY = PAY_B + 16
F32 = jnp.float32
BF16 = jnp.bfloat16


def dot(a, b):
    return jnp.dot(a, b, preferred_element_type=F32)


def dot_nt(a, b):
    return lax.dot_general(a, b, (((1,), (1,)), ((), ())), preferred_element_type=F32)


def iota(shape, axis):
    return lax.broadcasted_iota(jnp.int32, shape, axis)


def half_silu(h):
    return h * jnp.tanh(h) + h


def swap(a):
    return pltpu.roll(a, DH, axis=1)


def low_lanes(rows):
    return iota((rows, 128), 1) < DH


def join(lo, hi):
    return jnp.where(low_lanes(lo.shape[0]), lo, swap(hi))


def kernel(
    hist_in,
    length_in,
    bucket_in,
    cand_in,
    owner_in,
    weight_in,
    bias_in,
    gain_in,
    out_w_in,
    hist_out,
    cand_out,
    feats,
    weights,
    out_w,
    bucket_own,
    bucket_sib,
    cand_stack,
    cand_send,
    cand_arr,
    pay,
    got,
    gate_own,
    gate_send,
    gate_sib,
    queries,
    keys,
    values,
    back_c,
    back_h,
    arr_c,
    arr_h,
    done_stack,
    done_send,
    done_arr,
    local_sem,
    ring_s,
    ring_r,
    side_s,
    side_r,
    diag_s,
    diag_r,
    cand_s,
    cand_r,
    pay_s,
    pay_r,
    sib_s,
    sib_r,
    back_cs,
    back_cr,
    back_hs,
    back_hr,
    done_s,
    done_r,
):
    user = lax.axis_index("user")
    seq = lax.axis_index("seq")
    x, z = user // NZ, user % NZ
    y, core = seq // 2, seq % 2
    part = (x + z) % 4
    sibling = (user, y * 2 + (1 - core))

    def along_y(step):
        return (user, ((y + NY + step) % NY) * 2 + core)

    def along_x(step):
        return (((x + NX + step) % NX) * NZ + z, seq)

    def along_z(step):
        return (x * NZ + (z + NZ + step) % NZ, seq)

    def remote(src, dst, send, recv, to):
        return pltpu.make_async_remote_copy(
            src_ref=src, dst_ref=dst, send_sem=send, recv_sem=recv, device_id=to, device_id_type=MESH
        )

    own_weight = pltpu.make_async_copy(weight_in, weights.at[y], local_sem.at[0])
    own_feats = pltpu.make_async_copy(hist_in, feats.at[pl.ds(0, HR)], local_sem.at[1])
    own_out_w = pltpu.make_async_copy(out_w_in, out_w, local_sem.at[2])
    own_weight.start()
    own_feats.start()
    own_out_w.start()

    barrier = pltpu.get_barrier_semaphore()

    def greet_user(t, carry):
        pl.semaphore_signal(barrier, inc=1, device_id=((user + t) % NU, seq), device_id_type=MESH)
        return carry

    def greet_seq(t, carry):
        pl.semaphore_signal(barrier, inc=1, device_id=(user, (seq + t) % NS), device_id_type=MESH)
        return carry

    lax.fori_loop(1, NU, greet_user, 0)
    lax.fori_loop(1, NS, greet_seq, 0)

    lane = iota((32, 128), 1)
    row = iota((32, 128), 0)
    owner_row = jnp.concatenate([owner_in[...].astype(F32), jnp.zeros((1, 96), F32)], axis=1)
    owner_wide = jnp.broadcast_to(owner_row, (32, 128))
    owner_col = jnp.sum(jnp.where(lane == row, owner_wide, 0.0), axis=1, keepdims=True)
    same = (owner_wide == owner_col) & (lane < 32)
    rank_row = jnp.sum(jnp.where(same & (row < lane), 1.0, 0.0), axis=0, keepdims=True)
    rank_col = jnp.sum(jnp.where(same & (lane < row), 1.0, 0.0), axis=1, keepdims=True)
    slot_row = owner_row * 2.0 + rank_row
    slot_col = owner_col * 2.0 + rank_col
    spread = jnp.where(iota((128, 256), 0) == iota((128, 256), 1) % 32, 1.0, 0.0).astype(BF16)
    slot_wide = dot(jnp.broadcast_to(slot_row, (16, 128)).astype(BF16), spread)[0:1]
    for k in range(8):
        cand_stack[32 * k : 32 * k + 32, :] = cand_in[:, 128 * k : 128 * k + 128]
    m_row = iota((512, 256), 0)
    place = jnp.where(
        (m_row % 8 == iota((512, 256), 1) // 32) & ((m_row // 8).astype(F32) == slot_wide), 1.0, 0.0
    )
    cand_send[...] = dot(place.astype(BF16), cand_stack[...]).astype(BF16)
    bucket_own[...] = jnp.broadcast_to(bucket_in[...].astype(F32), (16, 128)).astype(BF16)

    pl.semaphore_wait(barrier, NU - 1 + NS - 1)

    sent = []

    def go(copy):
        copy.start()
        sent.append(copy)

    def quarter(origin, cls, half, at=0, rows=128):
        start = pl.multiple_of(cls * 256 + half * 128 + at, 64)
        return weights.at[origin, pl.ds(start, rows)]

    def ring_copy(dirn, step, half, src):
        sign = 1 if dirn == 0 else -1
        origin = (y + NY - sign * (step - 1)) % NY
        dst = quarter(origin, part, half)
        return remote(
            dst if src is None else src,
            dst,
            ring_s.at[dirn, step - 1, half],
            ring_r.at[dirn, step - 1, half],
            along_y(sign),
        )

    for half in range(2):
        start = pl.multiple_of(part * 256 + half * 128, 128)
        for dirn in range(2):
            go(ring_copy(dirn, 1, half, weight_in.at[pl.ds(start, 128)]))
    go(remote(hist_in, feats.at[pl.ds(HR, HR)], sib_s.at[0], sib_r.at[0], sibling))
    go(remote(bucket_own, bucket_sib, sib_s.at[1], sib_r.at[1], sibling))

    def cand_copy(t):
        to = (user + t) % NU
        return remote(
            cand_send.at[pl.ds(pl.multiple_of(to * 16, 16), 16)],
            cand_arr.at[pl.ds(pl.multiple_of(user * 16, 16), 16)],
            cand_s.at[t],
            cand_r.at[t],
            (to, seq),
        )

    def cand_start(t, carry):
        cand_copy(t).start()
        return carry

    lax.fori_loop(1, NU, cand_start, 0)
    mine = pl.ds(pl.multiple_of(user * 16, 16), 16)
    own_cand = pltpu.make_async_copy(cand_send.at[mine], cand_arr.at[mine], local_sem.at[3])
    own_cand.start()

    def origin_of(dirn, step):
        sign = 1 if dirn == 0 else -1
        return (y + NY - sign * step) % NY

    def index_of(dirn, step):
        return 2 * (step - 1) + (dirn if step < 4 else 0)

    def side_copy(dirn, step, axis, way):
        origin = origin_of(dirn, step)
        sign = 1 if way == 0 else -1
        ref = quarter(origin, part, axis)
        to = along_x(sign) if axis == 0 else along_z(sign)
        o = index_of(dirn, step)
        return remote(ref, ref, side_s.at[o, axis, way], side_r.at[o, axis, way], to)

    def diag_copy(dirn, step, axis, way):
        origin = origin_of(dirn, step)
        sign = 1 if way == 0 else -1
        ref = quarter(origin, (part + 4 - sign) % 4, axis, 64 * way, 64)
        to = along_x(sign) if axis == 0 else along_z(sign)
        o = index_of(dirn, step)
        return remote(ref, ref, diag_s.at[o, axis, way], diag_r.at[o, axis, way], to)

    def ring_step(step):
        for half in range(2):
            for dirn in range(2):
                if step == 4 and dirn != half:
                    continue
                ring_copy(dirn, step, half, None).wait_recv()
                if step < 3 or (step == 3 and dirn == half):
                    go(ring_copy(dirn, step + 1, half, None))
                for way in range(2):
                    go(side_copy(dirn, step, half, way))

    def side_step(step):
        for axis in range(2):
            for dirn in range(2 if step < 4 else 1):
                for way in range(2):
                    side_copy(dirn, step, axis, way).wait_recv()
                    go(diag_copy(dirn, step, axis, way))

    def diag_step(step):
        for axis in range(2):
            for dirn in range(2 if step < 4 else 1):
                for way in range(2):
                    diag_copy(dirn, step, axis, way).wait_recv()

    is_first = core == 0

    def project(origin, slot):
        acc = dot(feats[...], weights[origin])
        full = half_silu(acc * 0.5)
        gv, qk = full[:, 0:128], full[:, 128:256]
        gvb = gv.astype(BF16)
        gate_own[origin, 0:HR] = gvb[0:HR]
        gate_own[origin, HR : HR + CR] = gvb[2 * HR : 2 * HR + CR]
        gate_send[origin, 0:HR] = gvb[HR : 2 * HR]
        gate_send[origin, HR : HR + CR] = gvb[2 * HR + CR : 2 * HR + 2 * CR]
        at_own = pl.multiple_of(core * HR, HR)
        at_sib = pl.multiple_of((1 - core) * HR, HR)
        pay[slot, pl.ds(at_own, HR)] = qk[0:HR].astype(BF16)
        pay[slot, pl.ds(at_sib, HR)] = qk[HR : 2 * HR].astype(BF16)
        low = low_lanes(HR)
        own_v, sib_v = gv[0:HR], gv[HR : 2 * HR]
        v_pair = jnp.where(
            is_first, jnp.where(low, swap(own_v), sib_v), jnp.where(low, swap(sib_v), own_v)
        )
        pay[slot, PAY_V : PAY_V + HR] = v_pair.astype(BF16)
        own_q, sib_q = qk[2 * HR : 2 * HR + CR], qk[2 * HR + CR : 2 * HR + 2 * CR]
        q_pair = jnp.where(is_first, join(own_q, sib_q), join(sib_q, own_q))
        pay[slot, PAY_Q : PAY_Q + CR] = q_pair.astype(BF16)
        first = iota((16, 128), 0) == core
        pay[slot, PAY_B : PAY_B + 16] = jnp.where(
            first, bucket_own[...].astype(F32), bucket_sib[...].astype(F32)
        ).astype(BF16)

    def pay_copy(rel):
        to = (y + rel) % NY
        return remote(pay.at[rel], got.at[y], pay_s.at[rel], pay_r.at[rel], (user, to * 2 + core))

    def project_step(step):
        def one(k, carry):
            rel = jnp.where(k == 0, step, NY - step)
            project((y + rel) % NY, rel)
            pay_copy(rel).start()
            return carry

        lax.fori_loop(0, 2 if step < 4 else 1, one, 0)

    ring_step(1)

    def cand_wait(t, carry):
        cand_copy(t).wait_recv()
        return carry

    lax.fori_loop(1, NU, cand_wait, 0)
    own_cand.wait()
    col = iota((512, 512), 1)
    to_slots = jnp.where(col == 8 * (iota((512, 512), 0) % 64) + iota((512, 512), 0) // 64, 1.0, 0.0)
    slots = dot(to_slots.astype(BF16), cand_arr[...]).astype(BF16)
    for k in range(8):
        feats[2 * HR : 2 * HR + CR, 128 * k : 128 * k + 128] = slots[64 * k : 64 * k + 64]
    go(
        remote(
            feats.at[pl.ds(2 * HR, CR)],
            feats.at[pl.ds(2 * HR + CR, CR)],
            sib_s.at[2],
            sib_r.at[2],
            sibling,
        )
    )
    side_step(1)
    ring_step(2)

    own_feats.wait()
    own_weight.wait()
    remote(hist_in, feats.at[pl.ds(HR, HR)], sib_s.at[0], sib_r.at[0], sibling).wait_recv()
    remote(bucket_own, bucket_sib, sib_s.at[1], sib_r.at[1], sibling).wait_recv()
    remote(
        feats.at[pl.ds(2 * HR, CR)],
        feats.at[pl.ds(2 * HR + CR, CR)],
        sib_s.at[2],
        sib_r.at[2],
        sibling,
    ).wait_recv()
    project(y, 0)
    own_pay = pltpu.make_async_copy(pay.at[0], got.at[y], local_sem.at[4])
    own_pay.start()
    side_step(2)
    ring_step(3)
    diag_step(1)
    project_step(1)
    side_step(3)
    ring_step(4)
    diag_step(2)
    project_step(2)
    side_step(4)
    diag_step(3)
    project_step(3)
    diag_step(4)
    project_step(4)
    gate_copy = remote(gate_send, gate_sib, sib_s.at[3], sib_r.at[3], sibling)
    go(gate_copy)

    head_sel = iota((16, 128), 0) == seq
    table = jnp.concatenate([bias_in[...], jnp.zeros((16, 96), F32)], axis=1) * 0.5
    bias_row = jnp.sum(jnp.where(head_sel, table, 0.0), axis=0, keepdims=True)
    bias_hi = bias_row.astype(BF16).astype(F32)
    bias_lo = bias_row - bias_hi
    bias_lanes = pltpu.roll(jnp.broadcast_to(bias_hi, (8, 128)), DH, axis=1) + pltpu.roll(
        jnp.broadcast_to(bias_lo, (8, 128)), DH + NB, axis=1
    )
    bias_lanes = bias_lanes[0:1]
    length = length_in[0]

    own_pay.wait()

    def pay_wait(t, carry):
        pay_copy(t).wait_recv()
        return carry

    lax.fori_loop(1, NY, pay_wait, 0)

    low = low_lanes(HR)
    lane_h = iota((HR, 128), 1)
    row_h = iota((HR, 128), 0)

    def prepare(src, carry):
        v_pair = got[src, PAY_V : PAY_V + HR].astype(F32)
        v_swap = swap(v_pair)
        buckets = got[src, PAY_B : PAY_B + 16].astype(F32)
        base = src * (2 * HR)
        for c in range(2):
            qk = got[src, c * HR : c * HR + HR].astype(F32)
            at = pl.multiple_of(base + c * HR, HR)
            queries[pl.ds(at, HR)] = jnp.where(low, qk * 0.0625, bias_lanes).astype(BF16)
            mine_b = jnp.sum(jnp.where(lane_h == row_h, buckets[c : c + 1], 0.0), axis=1, keepdims=True)
            hit = jnp.where((lane_h % NB).astype(F32) == mine_b, 1.0, 0.0)
            keys[pl.ds(at, HR)] = jnp.where(low, swap(qk), hit).astype(BF16)
            v = jnp.where(low, v_pair, v_swap) if c == 0 else jnp.where(low, v_swap, v_pair)
            values[pl.ds(at, HR)] = jnp.where(row_h + at < length, v, 0.0).astype(BF16)
        q_pair = got[src, PAY_Q : PAY_Q + CR].astype(F32)
        low_c = low_lanes(CR)
        at = pl.multiple_of(HIST + src * HR, HR)
        queries[pl.ds(at, CR)] = jnp.where(low_c, q_pair * 0.0625, bias_lanes).astype(BF16)
        queries[pl.ds(at + CR, CR)] = jnp.where(low_c, swap(q_pair) * 0.0625, bias_lanes).astype(BF16)
        return carry

    lax.fori_loop(0, NY, prepare, 0)

    def attend(q, acc, at, width, mask=None):
        h = dot_nt(q, keys[pl.ds(at, width)])
        w = half_silu(h)
        if mask is not None:
            w = jnp.where(mask, w, 0.0)
        return acc + dot(w.astype(BF16), values[pl.ds(at, width)])

    def back_c_copy(to):
        return remote(
            back_c.at[to], arr_c.at[seq], back_cs.at[to], back_cr.at[seq], (user, to)
        )

    def back_h_copy(to):
        return remote(
            back_h.at[to], arr_h.at[seq], back_hs.at[to], back_hr.at[seq], (user, to)
        )

    def send_back(to, copy, out, arr):
        @pl.when(to != seq)
        def _():
            copy(to).start()

        @pl.when(to == seq)
        def _():
            arr[seq] = out

    def cand_block(i, carry):
        q = queries[pl.ds(pl.multiple_of(HIST + i * 256, 256), 256)]
        acc = jnp.zeros((256, 128), F32)
        for j in range(4):
            acc = attend(q, acc, 512 * j, 512)
        for c in range(4):
            o = acc[c * CR : c * CR + CR]
            packed = jnp.where(low_lanes(CR // 2), o[0 : CR // 2], o[CR // 2 : CR]).astype(BF16)
            to = i * 4 + c
            back_c[to] = packed
            send_back(to, back_c_copy, packed, arr_c)
        return carry

    lax.fori_loop(0, 4, cand_block, 0)

    tri = iota((256, 256), 1) <= iota((256, 256), 0)
    for i in range(8):
        q = queries[i * 256 : i * 256 + 256]
        acc = jnp.zeros((256, 128), F32)
        for j in range(i // 2):
            acc = attend(q, acc, 512 * j, 512)
        if i % 2:
            acc = attend(q, acc, (i - 1) * 256, 256)
        acc = attend(q, acc, i * 256, 256, tri)
        for c in range(2):
            o = acc[c * HR : c * HR + HR]
            packed = jnp.where(low_lanes(HR // 2), o[0 : HR // 2], o[HR // 2 : HR]).astype(BF16)
            to = i * 2 + c
            back_h[to] = packed
            send_back(to, back_h_copy, packed, arr_h)

    def wait_back(copy_sem, arr, back):
        def one(t, carry):
            src = (seq + t) % NS
            remote(back.at[src], arr.at[src], copy_sem[0].at[src], copy_sem[1].at[src], (user, src)).wait_recv()
            return carry

        lax.fori_loop(1, NS, one, 0)

    def finish(arr, rows, at, inputs):
        half = rows // 2
        low_half, low_rows = low_lanes(half), low_lanes(rows)
        tiles, total = [], jnp.zeros((rows, 128), F32)
        for p in range(NY):
            even, odd = arr[2 * p].astype(F32), arr[2 * p + 1].astype(F32)
            tile = jnp.concatenate(
                [jnp.where(low_half, even, swap(odd)), jnp.where(low_half, swap(even), odd)], axis=0
            )
            tiles.append(tile)
            total = total + tile
        mean = jnp.sum(total, axis=1, keepdims=True) * (1.0 / D)
        tiles = [t - mean for t in tiles]
        squares = jnp.zeros((rows, 128), F32)
        for t in tiles:
            squares = squares + t * t
        var = jnp.sum(squares, axis=1, keepdims=True) * (1.0 / D)
        scale = lax.rsqrt(var + NORM_EPS)
        gated = []
        for p in range(NY):
            own = gate_own[p, at : at + rows].astype(F32)
            sib = gate_sib[p, at : at + rows].astype(F32)
            even, odd = jnp.where(is_first, own, sib), jnp.where(is_first, sib, own)
            gate = jnp.where(low_rows, even, swap(odd))
            g = tiles[p] * scale * gain_in[:, 128 * p : 128 * p + 128] * gate
            gated.append(g.astype(BF16))
        result = dot(jnp.concatenate(gated, axis=1), out_w[...])
        return (result + inputs.astype(F32)).astype(BF16)

    gate_copy.wait_recv()
    own_out_w.wait()
    wait_back((back_cs, back_cr), arr_c, back_c)
    cand_done = finish(arr_c, CR, HR, feats[2 * HR : 2 * HR + CR])
    for k in range(8):
        done_stack[64 * k : 64 * k + 64] = cand_done[:, 128 * k : 128 * k + 128]
    r512 = iota((512, 512), 0)
    from_slots = jnp.where(r512 == 8 * (col % 64) + col // 64, 1.0, 0.0)
    done_send[...] = dot(from_slots.astype(BF16), done_stack[...]).astype(BF16)

    def done_copy(t):
        to = (user + t) % NU
        return remote(
            done_send.at[pl.ds(pl.multiple_of(to * 16, 16), 16)],
            done_arr.at[pl.ds(pl.multiple_of(user * 16, 16), 16)],
            done_s.at[t],
            done_r.at[t],
            (to, seq),
        )

    def done_start(t, carry):
        done_copy(t).start()
        return carry

    lax.fori_loop(1, NU, done_start, 0)
    own_done = pltpu.make_async_copy(done_send.at[mine], done_arr.at[mine], local_sem.at[5])
    own_done.start()

    wait_back((back_hs, back_hr), arr_h, back_h)
    hist_out[...] = finish(arr_h, HR, 0, feats[0:HR])

    def done_wait(t, carry):
        done_copy(t).wait_recv()
        return carry

    lax.fori_loop(1, NU, done_wait, 0)
    own_done.wait()
    slot_tall = jnp.concatenate([slot_col] * 8, axis=0)
    pick = jnp.where(
        iota((256, 512), 1).astype(F32) == slot_tall * 8.0 + (iota((256, 512), 0) // 32).astype(F32), 1.0, 0.0
    )
    picked = dot(pick.astype(BF16), done_arr[...]).astype(BF16)
    for k in range(8):
        cand_out[:, 128 * k : 128 * k + 128] = picked[32 * k : 32 * k + 32]

    for copy in sent:
        copy.wait_send()

    def user_sends(t, carry):
        cand_copy(t).wait_send()
        done_copy(t).wait_send()
        return carry

    def pay_sends(t, carry):
        pay_copy(t).wait_send()
        return carry

    def back_sends(t, carry):
        to = (seq + t) % NS
        back_c_copy(to).wait_send()
        back_h_copy(to).wait_send()
        return carry

    lax.fori_loop(1, NU, user_sends, 0)
    lax.fori_loop(1, NY, pay_sends, 0)
    lax.fori_loop(1, NS, back_sends, 0)


def body(hist, length, bucket, cand, owner, weight, bias, gain, out_weight):
    vmem = pl.BlockSpec(memory_space=pltpu.VMEM)
    hbm = pl.BlockSpec(memory_space=pl.ANY)
    smem = pl.BlockSpec(memory_space=pltpu.SMEM)
    dma = pltpu.SemaphoreType.DMA
    hist_out, cand_out = pl.pallas_call(
        kernel,
        out_shape=(
            jax.ShapeDtypeStruct((HR, D), BF16),
            jax.ShapeDtypeStruct((32, D), BF16),
        ),
        in_specs=[hbm, smem, vmem, vmem, vmem, hbm, vmem, vmem, hbm],
        out_specs=(vmem, vmem),
        scratch_shapes=[
            pltpu.VMEM((2 * HR + 2 * CR, D), BF16),
            pltpu.VMEM((NY, D, 4 * DH), BF16),
            pltpu.VMEM((D, D), BF16),
            pltpu.VMEM((16, 128), BF16),
            pltpu.VMEM((16, 128), BF16),
            pltpu.VMEM((256, 128), BF16),
            pltpu.VMEM((512, 128), BF16),
            pltpu.VMEM((512, 128), BF16),
            pltpu.VMEM((NY, PAY, 128), BF16),
            pltpu.VMEM((NY, PAY, 128), BF16),
            pltpu.VMEM((NY, HR + CR, 128), BF16),
            pltpu.VMEM((NY, HR + CR, 128), BF16),
            pltpu.VMEM((NY, HR + CR, 128), BF16),
            pltpu.VMEM((HIST + NS * CR, 128), BF16),
            pltpu.VMEM((HIST, 128), BF16),
            pltpu.VMEM((HIST, 128), BF16),
            pltpu.VMEM((NS, CR // 2, 128), BF16),
            pltpu.VMEM((NS, HR // 2, 128), BF16),
            pltpu.VMEM((NS, CR // 2, 128), BF16),
            pltpu.VMEM((NS, HR // 2, 128), BF16),
            pltpu.VMEM((512, 128), BF16),
            pltpu.VMEM((512, 128), BF16),
            pltpu.VMEM((512, 128), BF16),
            dma((6,)),
            dma((2, 4, 2)),
            dma((2, 4, 2)),
            dma((7, 2, 2)),
            dma((7, 2, 2)),
            dma((7, 2, 2)),
            dma((7, 2, 2)),
            dma((NU,)),
            dma((NU,)),
            dma((NY,)),
            dma((NY,)),
            dma((4,)),
            dma((4,)),
            dma((NS,)),
            dma((NS,)),
            dma((NS,)),
            dma((NS,)),
            dma((NU,)),
            dma((NU,)),
        ],
        compiler_params=pltpu.CompilerParams(
            collective_id=0, has_side_effects=True, vmem_limit_bytes=48 * 1024 * 1024
        ),
        cost_estimate=pl.CostEstimate(
            flops=4 * 10**9, bytes_accessed=8 * 10**6, transcendentals=5 * 10**6
        ),
    )(
        hist.reshape(HR, D),
        length,
        bucket,
        cand,
        owner.reshape(1, 32),
        weight.reshape(D, 4 * DH),
        bias,
        gain.reshape(1, D),
        out_weight,
    )
    return hist_out.reshape(1, HR, D), cand_out


def solution(mesh):
    in_specs = (
        P("user", "seq", None),
        P("user"),
        P("user", "seq"),
        P(("user", "seq"), None),
        P(("user", "seq"), None),
        P(None, "seq", None),
        P(),
        P(),
        P(),
    )
    out_specs = (P("user", "seq", None), P(("user", "seq"), None))
    return jax.shard_map(body, mesh=mesh, in_specs=in_specs, out_specs=out_specs, check_vma=False)
```

```python
import functools

import jax
import jax.numpy as jnp
from jax import lax
from jax.experimental import pallas as pl
from jax.experimental.pallas import tpu as pltpu
from jax.sharding import PartitionSpec as P

MESH = pl.DeviceIdType.MESH
NORM_EPS = 1e-05
NX, NZ, NY = 4, 8, 8
NU, NS = NX * NZ, NY * 2
D = 1024
DH = 64
NB = 32
HR = 128
CR = 64
HIST = HR * NS
PAY_V = 2 * HR
PAY_Q = 3 * HR
PAY_B = 3 * HR + CR
PAY = PAY_B + 16
F32 = jnp.float32
BF16 = jnp.bfloat16


def dot(a, b):
    return jnp.dot(a, b, preferred_element_type=F32)


def dot_nt(a, b):
    return lax.dot_general(a, b, (((1,), (1,)), ((), ())), preferred_element_type=F32)


def iota(shape, axis):
    return lax.broadcasted_iota(jnp.int32, shape, axis)


def half_silu(h):
    return h * jnp.tanh(h) + h


def swap(a):
    return pltpu.roll(a, DH, axis=1)


def low_lanes(rows):
    return iota((rows, 128), 1) < DH


def join(lo, hi):
    return jnp.where(low_lanes(lo.shape[0]), lo, swap(hi))


def kernel(
    hist_in,
    length_hbm,
    bucket_hbm,
    cand_hbm,
    owner_hbm,
    weight_in,
    bias_hbm,
    gain_hbm,
    out_w_in,
    hist_out,
    cand_out,
    length_in,
    bucket_in,
    cand_in,
    owner_in,
    bias_in,
    gain_in,
    feats,
    weights,
    out_w,
    bucket_own,
    bucket_sib,
    cand_send,
    cand_arr,
    pay,
    got,
    gate_own,
    gate_send,
    gate_sib,
    wide,
    queries,
    keys,
    values,
    acc,
    back_c,
    back_h,
    arr_c,
    arr_h,
    done_send,
    done_arr,
    local_sem,
    ring_s,
    ring_r,
    side_s,
    side_r,
    far_s,
    far_r,
    cand_s,
    cand_r,
    pay_s,
    pay_r,
    sib_s,
    sib_r,
    back_cs,
    back_cr,
    back_hs,
    back_hr,
    done_s,
    done_r,
):
    user = lax.axis_index("user")
    seq = lax.axis_index("seq")
    x, z = user // NZ, user % NZ
    y, core = seq // 2, seq % 2
    part = (x + z) % 4
    sibling = (user, y * 2 + (1 - core))

    def along_y(step):
        return (user, ((y + NY + step) % NY) * 2 + core)

    def along_x(step):
        return (((x + NX + step) % NX) * NZ + z, seq)

    def along_z(step):
        return (x * NZ + (z + NZ + step) % NZ, seq)

    def remote(src, dst, send, recv, to):
        return pltpu.make_async_remote_copy(
            src_ref=src, dst_ref=dst, send_sem=send, recv_sem=recv, device_id=to, device_id_type=MESH
        )

    barrier = pltpu.get_barrier_semaphore()

    def greet_user(t, carry):
        pl.semaphore_signal(barrier, inc=1, device_id=((user + t) % NU, seq), device_id_type=MESH)
        return carry

    def greet_seq(t, carry):
        pl.semaphore_signal(barrier, inc=1, device_id=(user, (seq + t) % NS), device_id_type=MESH)
        return carry

    lax.fori_loop(1, NU, greet_user, 0)
    lax.fori_loop(1, NS, greet_seq, 0)

    own_weight = pltpu.make_async_copy(weight_in, weights.at[y], local_sem.at[0])
    own_feats = pltpu.make_async_copy(hist_in, feats.at[pl.ds(0, HR)], local_sem.at[1])
    own_out_w = pltpu.make_async_copy(out_w_in, out_w, local_sem.at[2])
    small = [
        pltpu.make_async_copy(src, dst, local_sem.at[6 + n])
        for n, (src, dst) in enumerate(
            (
                (owner_hbm, owner_in),
                (cand_hbm, cand_in),
                (bucket_hbm, bucket_in),
                (length_hbm, length_in),
                (bias_hbm, bias_in),
                (gain_hbm, gain_in),
            )
        )
    ]
    for copy in small:
        copy.start()
    own_weight.start()
    own_feats.start()
    own_out_w.start()

    pl.semaphore_wait(barrier, NU - 1 + NS - 1)

    sent = []

    def go(copy):
        copy.start()
        sent.append(copy)

    def quarter(origin, cls, half, at=0, rows=128):
        start = pl.multiple_of(cls * 256 + half * 128 + at, 64)
        return weights.at[origin, pl.ds(start, rows)]

    def ring_copy(dirn, step, half, src):
        sign = 1 if dirn == 0 else -1
        origin = (y + NY - sign * (step - 1)) % NY
        dst = quarter(origin, part, half)
        return remote(
            dst if src is None else src,
            dst,
            ring_s.at[dirn, step - 1, half],
            ring_r.at[dirn, step - 1, half],
            along_y(sign),
        )

    for half in range(2):
        start = pl.multiple_of(part * 256 + half * 128, 128)
        for dirn in range(2):
            go(ring_copy(dirn, 1, half, weight_in.at[pl.ds(start, 128)]))
    go(remote(hist_in, feats.at[pl.ds(HR, HR)], sib_s.at[0], sib_r.at[0], sibling))

    for copy in small:
        copy.wait()
    lane = iota((32, 128), 1)
    row = iota((32, 128), 0)
    owner_row = jnp.concatenate([owner_in[...].astype(F32), jnp.zeros((1, 96), F32)], axis=1)
    owner_wide = jnp.broadcast_to(owner_row, (32, 128))
    owner_col = jnp.sum(jnp.where(lane == row, owner_wide, 0.0), axis=1, keepdims=True)
    same = (owner_wide == owner_col) & (lane < 32)
    rank_row = jnp.sum(jnp.where(same & (row < lane), 1.0, 0.0), axis=0, keepdims=True)
    rank_col = jnp.sum(jnp.where(same & (lane < row), 1.0, 0.0), axis=1, keepdims=True)
    slot_row = owner_row * 2.0 + rank_row
    slot_col = owner_col * 2.0 + rank_col

    def split_rows(slots, out):
        for k in range(8):
            wide[pl.ds(k, CR, stride=8), :] = slots[:, 128 * k : 128 * k + 128]
        out[...] = wide[...].astype(BF16)

    def join_rows(arrived):
        wide[...] = arrived[...].astype(F32)
        return [wide[pl.ds(k, CR, stride=8), :].astype(BF16) for k in range(8)]

    put = jnp.where(iota((CR, 32), 0).astype(F32) == slot_row[:, 0:32], 1.0, 0.0).astype(BF16)
    split_rows(dot(put, cand_in[...]), cand_send)
    bucket_own[...] = jnp.broadcast_to(bucket_in[...].astype(F32), (16, 128)).astype(BF16)
    go(remote(bucket_own, bucket_sib, sib_s.at[1], sib_r.at[1], sibling))

    def cand_copy(t):
        to = (user + t) % NU
        return remote(
            cand_send.at[pl.ds(pl.multiple_of(to * 16, 16), 16)],
            cand_arr.at[pl.ds(pl.multiple_of(user * 16, 16), 16)],
            cand_s.at[t],
            cand_r.at[t],
            (to, seq),
        )

    def cand_start(t, carry):
        cand_copy(t).start()
        return carry

    lax.fori_loop(1, NU, cand_start, 0)
    mine = pl.ds(pl.multiple_of(user * 16, 16), 16)
    own_cand = pltpu.make_async_copy(cand_send.at[mine], cand_arr.at[mine], local_sem.at[3])
    own_cand.start()

    def origin_of(dirn, step):
        sign = 1 if dirn == 0 else -1
        return (y + NY - sign * step) % NY

    def index_of(dirn, step):
        return 2 * (step - 1) + (dirn if step < 4 else 0)

    def side_copy(dirn, step, half, way):
        ref = quarter(origin_of(dirn, step), part, half)
        o = index_of(dirn, step)
        to = along_x(1 if way == 0 else -1)
        return remote(ref, ref, side_s.at[o, half, way], side_r.at[o, half, way], to)

    def far_copy(dirn, step, half):
        ref = quarter(origin_of(dirn, step), part, half)
        o = index_of(dirn, step)
        to = along_z(2 if half == 0 else -2)
        return remote(ref, ref, far_s.at[o, half], far_r.at[o, half], to)

    def ring_step(step):
        for half in range(2):
            for dirn in range(2):
                if step == 4 and dirn != half:
                    continue
                ring_copy(dirn, step, half, None).wait_recv()
                if step < 3 or (step == 3 and dirn == half):
                    go(ring_copy(dirn, step + 1, half, None))
                for way in range(2):
                    go(side_copy(dirn, step, half, way))
                go(far_copy(dirn, step, half))

    def side_step(step):
        for half in range(2):
            for dirn in range(2 if step < 4 else 1):
                for way in range(2):
                    side_copy(dirn, step, half, way).wait_recv()
                far_copy(dirn, step, half).wait_recv()

    is_first = core == 0

    def project(origin, slot):
        acc = dot(feats[...], weights[origin])
        full = half_silu(acc * 0.5)
        gv, qk = full[:, 0:128], full[:, 128:256]
        gvb = gv.astype(BF16)
        gate_own[origin, 0:HR] = gvb[0:HR]
        gate_own[origin, HR : HR + CR] = gvb[2 * HR : 2 * HR + CR]
        gate_send[origin, 0:HR] = gvb[HR : 2 * HR]
        gate_send[origin, HR : HR + CR] = gvb[2 * HR + CR : 2 * HR + 2 * CR]
        at_own = pl.multiple_of(core * HR, HR)
        at_sib = pl.multiple_of((1 - core) * HR, HR)
        pay[slot, pl.ds(at_own, HR)] = qk[0:HR].astype(BF16)
        pay[slot, pl.ds(at_sib, HR)] = qk[HR : 2 * HR].astype(BF16)
        low = low_lanes(HR)
        own_v, sib_v = gv[0:HR], gv[HR : 2 * HR]
        v_pair = jnp.where(
            is_first, jnp.where(low, swap(own_v), sib_v), jnp.where(low, swap(sib_v), own_v)
        )
        pay[slot, PAY_V : PAY_V + HR] = v_pair.astype(BF16)
        own_q, sib_q = qk[2 * HR : 2 * HR + CR], qk[2 * HR + CR : 2 * HR + 2 * CR]
        q_pair = jnp.where(is_first, join(own_q, sib_q), join(sib_q, own_q))
        pay[slot, PAY_Q : PAY_Q + CR] = q_pair.astype(BF16)
        first = iota((16, 128), 0) == core
        pay[slot, PAY_B : PAY_B + 16] = jnp.where(
            first, bucket_own[...].astype(F32), bucket_sib[...].astype(F32)
        ).astype(BF16)

    def pay_copy(rel):
        to = (y + rel + NY // 2) % NY
        return remote(pay.at[rel], got.at[y], pay_s.at[rel], pay_r.at[rel], (user, to * 2 + core))

    def project_step(step):
        def one(k, carry):
            rel = jnp.where(k == 0, step, NY - step)
            project((y + rel) % NY, rel)
            pay_copy(rel).start()
            return carry

        lax.fori_loop(0, 2, one, 0)

    ring_step(1)

    def cand_wait(t, carry):
        cand_copy(t).wait_recv()
        return carry

    lax.fori_loop(1, NU, cand_wait, 0)
    own_cand.wait()
    for k, columns in enumerate(join_rows(cand_arr)):
        feats[2 * HR : 2 * HR + CR, 128 * k : 128 * k + 128] = columns
    go(
        remote(
            feats.at[pl.ds(2 * HR, CR)],
            feats.at[pl.ds(2 * HR + CR, CR)],
            sib_s.at[2],
            sib_r.at[2],
            sibling,
        )
    )
    ring_step(2)

    own_feats.wait()
    own_weight.wait()
    remote(hist_in, feats.at[pl.ds(HR, HR)], sib_s.at[0], sib_r.at[0], sibling).wait_recv()
    remote(bucket_own, bucket_sib, sib_s.at[1], sib_r.at[1], sibling).wait_recv()
    remote(
        feats.at[pl.ds(2 * HR, CR)],
        feats.at[pl.ds(2 * HR + CR, CR)],
        sib_s.at[2],
        sib_r.at[2],
        sibling,
    ).wait_recv()
    project(y, 0)
    pay_copy(0).start()
    head_sel = iota((16, 128), 0) == 2 * ((y + NY // 2) % NY) + core
    table = jnp.concatenate([bias_in[...], jnp.zeros((16, 96), F32)], axis=1) * 0.5
    bias_row = jnp.sum(jnp.where(head_sel, table, 0.0), axis=0, keepdims=True)
    bias_hi = bias_row.astype(BF16).astype(F32)
    bias_lo = bias_row - bias_hi
    bias_lanes = pltpu.roll(jnp.broadcast_to(bias_hi, (8, 128)), DH, axis=1) + pltpu.roll(
        jnp.broadcast_to(bias_lo, (8, 128)), DH + NB, axis=1
    )
    bias_lanes = bias_lanes[0:1]
    length = length_in[0]

    low = low_lanes(HR)
    lane_h = iota((HR, 128), 1)
    row_h = iota((HR, 128), 0)

    def prepare(src):
        v_pair = got[src, PAY_V : PAY_V + HR].astype(F32)
        v_swap = swap(v_pair)
        buckets = got[src, PAY_B : PAY_B + 16].astype(F32)
        base = src * (2 * HR)
        for c in range(2):
            qk = got[src, c * HR : c * HR + HR].astype(F32)
            at = c * HR
            queries[src, at : at + HR] = jnp.where(low, qk * 0.0625, bias_lanes).astype(BF16)
            mine_b = jnp.sum(jnp.where(lane_h == row_h, buckets[c : c + 1], 0.0), axis=1, keepdims=True)
            hit = jnp.where((lane_h & (NB - 1)).astype(F32) == mine_b, 1.0, 0.0)
            keys[src, at : at + HR] = jnp.where(low, swap(qk), hit).astype(BF16)
            v = jnp.where(low, v_pair, v_swap) if c == 0 else jnp.where(low, v_swap, v_pair)
            values[src, at : at + HR] = jnp.where(row_h + (base + at) < length, v, 0.0).astype(BF16)
        q_pair = got[src, PAY_Q : PAY_Q + CR].astype(F32)
        low_c = low_lanes(CR)
        at = 2 * HR
        queries[src, at : at + CR] = jnp.where(low_c, q_pair * 0.0625, bias_lanes).astype(BF16)
        queries[src, at + CR : at + 2 * CR] = jnp.where(low_c, swap(q_pair) * 0.0625, bias_lanes).astype(BF16)

    def source(m):
        return (y + NY // 2 + jnp.where(m % 2 == 1, (m + 1) // 2, NY - m // 2)) % NY

    def weigh(q, src, mask=None):
        w = half_silu(dot_nt(q, keys[src]))
        if mask is not None:
            w = jnp.where(mask, w, 0.0)
        return dot(w.astype(BF16), values[src])

    def take_in(*new):
        for m in new:
            prepare(source(m))
        tri = iota((2 * HR + 2 * CR, 2 * HR), 1) <= iota((2 * HR + 2 * CR, 2 * HR), 0)
        own = [source(m) for m in new]
        for n, part_sum in [(n, weigh(queries[n], n, tri)) for n in own]:
            acc[n] = part_sum
        pairs = [(source(m), source(k)) for m in new for k in range(m)]
        for at in range(0, len(pairs), 4):
            sums = []
            for n, a in pairs[at : at + 4]:
                later, earlier = jnp.where(a < n, n, a), jnp.where(a < n, a, n)
                sums.append((later, 0, weigh(queries[later], earlier)))
                sums.append((earlier, 2 * HR, weigh(queries[earlier, 2 * HR :], later)))
            for src, first, part_sum in sums:
                acc[src, first:] += part_sum

    def take_in_step(step):
        pay_copy(NY - step).wait_recv()
        pay_copy(step).wait_recv()
        take_in(2 * step - 1, 2 * step)

    def back_c_copy(to):
        return remote(
            back_c.at[to], arr_c.at[seq], back_cs.at[to], back_cr.at[seq], (user, to)
        )

    def back_h_copy(to):
        return remote(
            back_h.at[to], arr_h.at[seq], back_hs.at[to], back_hr.at[seq], (user, to)
        )

    def send_back(to, copy, out, arr):
        @pl.when(to != seq)
        def _():
            copy(to).start()

        @pl.when(to == seq)
        def _():
            arr[seq] = out

    def send_cands(i, carry):
        for c in range(2):
            at = 2 * HR + c * CR
            lo, hi = acc[i, at : at + CR // 2], acc[i, at + CR // 2 : at + CR]
            packed = jnp.where(low_lanes(CR // 2), lo, hi).astype(BF16)
            to = i * 2 + c
            back_c[to] = packed
            send_back(to, back_c_copy, packed, arr_c)
        return carry

    def send_hist(i, carry):
        for c in range(2):
            at = c * HR
            lo, hi = acc[i, at : at + HR // 2], acc[i, at + HR // 2 : at + HR]
            packed = jnp.where(low_lanes(HR // 2), lo, hi).astype(BF16)
            to = i * 2 + c
            back_h[to] = packed
            send_back(to, back_h_copy, packed, arr_h)
        return carry

    side_step(1)
    project_step(1)
    ring_step(3)
    side_step(2)
    project_step(2)
    ring_step(4)
    side_step(3)
    project_step(3)
    pay_copy(0).wait_recv()
    take_in(0)
    take_in_step(1)
    side_step(4)
    project((y + 4) % NY, 4)
    own_pay = pltpu.make_async_copy(pay.at[4], got.at[y], local_sem.at[4])
    own_pay.start()
    gate_copy = remote(gate_send, gate_sib, sib_s.at[3], sib_r.at[3], sibling)
    go(gate_copy)
    take_in_step(2)
    take_in_step(3)
    last = source(7)
    lax.fori_loop(0, last, send_hist, 0)
    own_pay.wait()
    take_in(7)
    lax.fori_loop(0, NY, send_cands, 0)
    lax.fori_loop(last, NY, send_hist, 0)

    def wait_back(copy_sem, arr, back):
        def one(t, carry):
            src = (seq + t) % NS
            remote(back.at[src], arr.at[src], copy_sem[0].at[src], copy_sem[1].at[src], (user, src)).wait_recv()
            return carry

        lax.fori_loop(1, NS, one, 0)

    def finish(arr, rows, at, inputs):
        half = rows // 2
        low_half, low_rows = low_lanes(half), low_lanes(rows)
        tiles, total = [], jnp.zeros((rows, 128), F32)
        for p in range(NY):
            at_p = 2 * ((p + NY // 2) % NY)
            even, odd = arr[at_p].astype(F32), arr[at_p + 1].astype(F32)
            tile = jnp.concatenate(
                [jnp.where(low_half, even, swap(odd)), jnp.where(low_half, swap(even), odd)], axis=0
            )
            tiles.append(tile)
            total = total + tile
        mean = jnp.sum(total, axis=1, keepdims=True) * (1.0 / D)
        tiles = [t - mean for t in tiles]
        squares = jnp.zeros((rows, 128), F32)
        for t in tiles:
            squares = squares + t * t
        var = jnp.sum(squares, axis=1, keepdims=True) * (1.0 / D)
        scale = lax.rsqrt(var + NORM_EPS)
        gated = []
        for p in range(NY):
            own = gate_own[p, at : at + rows].astype(F32)
            sib = gate_sib[p, at : at + rows].astype(F32)
            even, odd = jnp.where(is_first, own, sib), jnp.where(is_first, sib, own)
            gate = jnp.where(low_rows, even, swap(odd))
            g = tiles[p] * scale * gain_in[:, 128 * p : 128 * p + 128] * gate
            gated.append(g.astype(BF16))
        result = dot(jnp.concatenate(gated, axis=1), out_w[...])
        return result + inputs.astype(F32)

    gate_copy.wait_recv()
    own_out_w.wait()
    wait_back((back_cs, back_cr), arr_c, back_c)
    cand_done = finish(arr_c, CR, HR, feats[2 * HR : 2 * HR + CR])
    split_rows(cand_done, done_send)

    def done_copy(t):
        to = (user + t) % NU
        return remote(
            done_send.at[pl.ds(pl.multiple_of(to * 16, 16), 16)],
            done_arr.at[pl.ds(pl.multiple_of(user * 16, 16), 16)],
            done_s.at[t],
            done_r.at[t],
            (to, seq),
        )

    def done_start(t, carry):
        done_copy(t).start()
        return carry

    lax.fori_loop(1, NU, done_start, 0)
    own_done = pltpu.make_async_copy(done_send.at[mine], done_arr.at[mine], local_sem.at[5])
    own_done.start()

    wait_back((back_hs, back_hr), arr_h, back_h)
    hist_out[...] = finish(arr_h, HR, 0, feats[0:HR]).astype(BF16)

    def done_wait(t, carry):
        done_copy(t).wait_recv()
        return carry

    lax.fori_loop(1, NU, done_wait, 0)
    own_done.wait()
    pick = jnp.where(iota((32, CR), 1).astype(F32) == slot_col, 1.0, 0.0).astype(BF16)
    for k, columns in enumerate(join_rows(done_arr)):
        cand_out[:, 128 * k : 128 * k + 128] = dot(pick, columns).astype(BF16)

    for copy in sent:
        copy.wait_send()

    def user_sends(t, carry):
        cand_copy(t).wait_send()
        done_copy(t).wait_send()
        return carry

    def pay_sends(t, carry):
        pay_copy((t + 4) % NY).wait_send()
        return carry

    def back_sends(t, carry):
        to = (seq + t) % NS
        back_c_copy(to).wait_send()
        back_h_copy(to).wait_send()
        return carry

    lax.fori_loop(1, NU, user_sends, 0)
    lax.fori_loop(1, NY, pay_sends, 0)
    lax.fori_loop(1, NS, back_sends, 0)


def body(hist, length, bucket, cand, owner, weight, bias, gain, out_weight):
    vmem = pl.BlockSpec(memory_space=pltpu.VMEM)
    hbm = pl.BlockSpec(memory_space=pltpu.HBM)
    dma = pltpu.SemaphoreType.DMA
    hist_out, cand_out = pl.pallas_call(
        kernel,
        out_shape=(
            jax.ShapeDtypeStruct((HR, D), BF16),
            jax.ShapeDtypeStruct((32, D), BF16),
        ),
        in_specs=[hbm] * 9,
        out_specs=(vmem, vmem),
        scratch_shapes=[
            pltpu.SMEM((1,), jnp.int32),
            pltpu.VMEM((1, 128), jnp.int32),
            pltpu.VMEM((32, D), BF16),
            pltpu.VMEM((1, 32), jnp.int32),
            pltpu.VMEM((NS, NB), F32),
            pltpu.VMEM((1, D), F32),
            pltpu.VMEM((2 * HR + 2 * CR, D), BF16),
            pltpu.VMEM((NY, D, 4 * DH), BF16),
            pltpu.VMEM((D, D), BF16),
            pltpu.VMEM((16, 128), BF16),
            pltpu.VMEM((16, 128), BF16),
            pltpu.VMEM((512, 128), BF16),
            pltpu.VMEM((512, 128), BF16),
            pltpu.VMEM((NY, PAY, 128), BF16),
            pltpu.VMEM((NY, PAY, 128), BF16),
            pltpu.VMEM((NY, HR + CR, 128), BF16),
            pltpu.VMEM((NY, HR + CR, 128), BF16),
            pltpu.VMEM((NY, HR + CR, 128), BF16),
            pltpu.VMEM((512, 128), F32),
            pltpu.VMEM((NY, 2 * HR + 2 * CR, 128), BF16),
            pltpu.VMEM((NY, 2 * HR, 128), BF16),
            pltpu.VMEM((NY, 2 * HR, 128), BF16),
            pltpu.VMEM((NY, 2 * HR + 2 * CR, 128), F32),
            pltpu.VMEM((NS, CR // 2, 128), BF16),
            pltpu.VMEM((NS, HR // 2, 128), BF16),
            pltpu.VMEM((NS, CR // 2, 128), BF16),
            pltpu.VMEM((NS, HR // 2, 128), BF16),
            pltpu.VMEM((512, 128), BF16),
            pltpu.VMEM((512, 128), BF16),
            dma((12,)),
            dma((2, 4, 2)),
            dma((2, 4, 2)),
            dma((7, 2, 2)),
            dma((7, 2, 2)),
            dma((7, 2)),
            dma((7, 2)),
            dma((NU,)),
            dma((NU,)),
            dma((NY,)),
            dma((NY,)),
            dma((4,)),
            dma((4,)),
            dma((NS,)),
            dma((NS,)),
            dma((NS,)),
            dma((NS,)),
            dma((NU,)),
            dma((NU,)),
        ],
        compiler_params=pltpu.CompilerParams(
            collective_id=0, has_side_effects=True, vmem_limit_bytes=60 * 1024 * 1024
        ),
        cost_estimate=pl.CostEstimate(
            flops=4 * 10**9, bytes_accessed=8 * 10**6, transcendentals=5 * 10**6
        ),
    )(
        hist.reshape(HR, D),
        length,
        bucket,
        cand,
        owner.reshape(1, 32),
        weight.reshape(D, 4 * DH),
        bias,
        gain.reshape(1, D),
        out_weight,
    )
    return hist_out.reshape(1, HR, D), cand_out


def solution(mesh):
    in_specs = (
        P("user", "seq", None),
        P("user"),
        P("user", "seq"),
        P(("user", "seq"), None),
        P(("user", "seq"), None),
        P(None, "seq", None),
        P(),
        P(),
        P(),
    )
    out_specs = (P("user", "seq", None), P(("user", "seq"), None))
    return jax.shard_map(body, mesh=mesh, in_specs=in_specs, out_specs=out_specs, check_vma=False)
```

```python
import functools

import jax
import jax.numpy as jnp
from jax import lax
from jax.experimental import pallas as pl
from jax.experimental.pallas import tpu as pltpu
from jax.sharding import PartitionSpec as P

MESH = pl.DeviceIdType.MESH
NORM_EPS = 1e-05
NX, NZ, NY = 4, 8, 8
NU, NS = NX * NZ, NY * 2
D = 1024
DH = 64
NB = 32
HR = 128
CR = 64
HIST = HR * NS
PAY_V = 2 * HR
PAY_B = 3 * HR
PAY_Q = PAY_B + 16
PAY = PAY_Q + CR
F32 = jnp.float32
BF16 = jnp.bfloat16


def dot(a, b):
    return jnp.dot(a, b, preferred_element_type=F32)


def dot_nt(a, b):
    return lax.dot_general(a, b, (((1,), (1,)), ((), ())), preferred_element_type=F32)


def iota(shape, axis):
    return lax.broadcasted_iota(jnp.int32, shape, axis)


def half_silu(h):
    return h * jnp.tanh(h) + h


def swap(a):
    return pltpu.roll(a, DH, axis=1)


def low_lanes(rows):
    return iota((rows, 128), 1) < DH


def join(lo, hi):
    return jnp.where(low_lanes(lo.shape[0]), lo, swap(hi))


def kernel(
    hist_in,
    length_hbm,
    bucket_hbm,
    cand_hbm,
    owner_hbm,
    weight_in,
    bias_hbm,
    gain_hbm,
    out_w_in,
    hist_out,
    cand_out,
    hist_done,
    gain_gate,
    length_in,
    bucket_in,
    cand_in,
    owner_in,
    bias_in,
    gain_in,
    feats,
    weights,
    out_w,
    bucket_own,
    bucket_sib,
    cand_send,
    cand_arr,
    pay,
    got,
    gate_own,
    gate_send,
    gate_sib,
    wide,
    queries,
    keys,
    values,
    acc,
    back_c,
    back_h,
    arr_c,
    arr_h,
    done_send,
    done_arr,
    local_sem,
    ring_s,
    ring_r,
    side_s,
    side_r,
    far_s,
    far_r,
    cand_s,
    cand_r,
    pay_s,
    pay_r,
    sib_s,
    sib_r,
    back_cs,
    back_cr,
    back_hs,
    back_hr,
    done_s,
    done_r,
):
    user = lax.axis_index("user")
    seq = lax.axis_index("seq")
    x, z = user // NZ, user % NZ
    y, core = seq // 2, seq % 2
    part = (x + z) % 4
    sibling = (user, y * 2 + (1 - core))

    def along_y(step):
        return (user, ((y + NY + step) % NY) * 2 + core)

    def along_x(step):
        return (((x + NX + step) % NX) * NZ + z, seq)

    def along_z(step):
        return (x * NZ + (z + NZ + step) % NZ, seq)

    def remote(src, dst, send, recv, to):
        return pltpu.make_async_remote_copy(
            src_ref=src, dst_ref=dst, send_sem=send, recv_sem=recv, device_id=to, device_id_type=MESH
        )

    barrier = pltpu.get_barrier_semaphore()

    def greet_user(t, carry):
        pl.semaphore_signal(barrier, inc=1, device_id=((user + t) % NU, seq), device_id_type=MESH)
        return carry

    def greet_seq(t, carry):
        pl.semaphore_signal(barrier, inc=1, device_id=(user, (seq + t) % NS), device_id_type=MESH)
        return carry

    lax.fori_loop(1, NU, greet_user, 0)
    lax.fori_loop(1, NS, greet_seq, 0)

    own_weight = pltpu.make_async_copy(weight_in, weights.at[y], local_sem.at[0])
    own_feats = pltpu.make_async_copy(hist_in, feats.at[pl.ds(0, HR)], local_sem.at[1])
    own_out_w = pltpu.make_async_copy(out_w_in, out_w, local_sem.at[2])
    small = [
        pltpu.make_async_copy(src, dst, local_sem.at[6 + n])
        for n, (src, dst) in enumerate(
            (
                (owner_hbm, owner_in),
                (cand_hbm, cand_in),
                (bucket_hbm, bucket_in),
                (length_hbm, length_in),
                (bias_hbm, bias_in),
                (gain_hbm, gain_in),
            )
        )
    ]
    for copy in small:
        copy.start()
    own_weight.start()
    own_feats.start()
    own_out_w.start()

    for copy in small:
        copy.wait()
    lane = iota((32, 128), 1)
    row = iota((32, 128), 0)
    owner_row = jnp.concatenate([owner_in[...].astype(F32), jnp.zeros((1, 96), F32)], axis=1)
    owner_wide = jnp.broadcast_to(owner_row, (32, 128))
    owner_col = jnp.sum(jnp.where(lane == row, owner_wide, 0.0), axis=1, keepdims=True)
    same = (owner_wide == owner_col) & (lane < 32)
    rank_row = jnp.sum(jnp.where(same & (row < lane), 1.0, 0.0), axis=0, keepdims=True)
    rank_col = jnp.sum(jnp.where(same & (lane < row), 1.0, 0.0), axis=1, keepdims=True)
    slot_row = owner_row * 2.0 + rank_row
    slot_col = owner_col * 2.0 + rank_col

    def split_rows(slots, out):
        for k in range(8):
            wide[pl.ds(k, CR, stride=8), :] = slots[:, 128 * k : 128 * k + 128]
        out[...] = wide[...].astype(BF16)

    def join_rows(arrived):
        wide[...] = arrived[...].astype(F32)
        return [wide[pl.ds(k, CR, stride=8), :].astype(BF16) for k in range(8)]

    put = jnp.where(iota((CR, 32), 0).astype(F32) == slot_row[:, 0:32], 1.0, 0.0).astype(BF16)
    split_rows(dot(put, cand_in[...]), cand_send)
    bucket_own[...] = jnp.broadcast_to(bucket_in[...].astype(F32), (16, 128)).astype(BF16)

    pl.semaphore_wait(barrier, NU - 1 + NS - 1)

    sent = []

    def go(copy):
        copy.start()
        sent.append(copy)

    def quarter(origin, cls, half, at=0, rows=128):
        start = pl.multiple_of(cls * 256 + half * 128 + at, 64)
        return weights.at[origin, pl.ds(start, rows)]

    def ring_copy(dirn, step, piece, src):
        sign = 1 if dirn == 0 else -1
        origin = (y + NY - sign * (step - 1)) % NY
        dst = quarter(origin, part, piece // 2, 64 * (piece % 2), 64)
        return remote(
            dst if src is None else src,
            dst,
            ring_s.at[dirn, step - 1, piece],
            ring_r.at[dirn, step - 1, piece],
            along_y(sign),
        )

    for piece in range(4):
        start = pl.multiple_of(part * 256 + piece * 64, 64)
        for dirn in range(2):
            go(ring_copy(dirn, 1, piece, weight_in.at[pl.ds(start, 64)]))
    go(remote(hist_in, feats.at[pl.ds(HR, HR)], sib_s.at[0], sib_r.at[0], sibling))

    go(remote(bucket_own, bucket_sib, sib_s.at[1], sib_r.at[1], sibling))

    def cand_copy(t):
        to = (user + t) % NU
        return remote(
            cand_send.at[pl.ds(pl.multiple_of(to * 16, 16), 16)],
            cand_arr.at[pl.ds(pl.multiple_of(user * 16, 16), 16)],
            cand_s.at[t],
            cand_r.at[t],
            (to, seq),
        )

    def cand_start(t, carry):
        cand_copy(t).start()
        return carry

    lax.fori_loop(1, NU, cand_start, 0)
    mine = pl.ds(pl.multiple_of(user * 16, 16), 16)
    own_cand = pltpu.make_async_copy(cand_send.at[mine], cand_arr.at[mine], local_sem.at[3])
    own_cand.start()

    def origin_of(dirn, step):
        sign = 1 if dirn == 0 else -1
        return (y + NY - sign * step) % NY

    def index_of(dirn, step):
        return 2 * (step - 1) + (dirn if step < 4 else 0)

    def side_copy(dirn, step, half, way):
        ref = quarter(origin_of(dirn, step), part, half)
        o = index_of(dirn, step)
        to = along_x(1 if way == 0 else -1)
        return remote(ref, ref, side_s.at[o, half, way], side_r.at[o, half, way], to)

    def far_copy(dirn, step, half):
        ref = quarter(origin_of(dirn, step), part, half)
        o = index_of(dirn, step)
        to = along_z(2 if half == 0 else -2)
        return remote(ref, ref, far_s.at[o, half], far_r.at[o, half], to)

    def ring_step(step):
        for half in range(2):
            for dirn in range(2):
                if step == 4 and dirn != half:
                    continue
                for piece in (2 * half, 2 * half + 1):
                    ring_copy(dirn, step, piece, None).wait_recv()
                    if step < 3 or (step == 3 and dirn == half):
                        go(ring_copy(dirn, step + 1, piece, None))
                for way in range(2):
                    go(side_copy(dirn, step, half, way))
                go(far_copy(dirn, step, half))

    def side_step(step):
        for half in range(2):
            for dirn in range(2 if step < 4 else 1):
                for way in range(2):
                    side_copy(dirn, step, half, way).wait_recv()
                far_copy(dirn, step, half).wait_recv()

    is_first = core == 0

    def project(*heads):
        sums = [dot(feats[...], weights[origin]) for origin, slot in heads]
        for (origin, slot), part_sum in zip(heads, sums):
            full = half_silu(part_sum * 0.5)
            pack_hist(origin, slot, full[0 : 2 * HR])
            pack_cand(origin, slot, full[2 * HR :])

    def pack_hist(origin, slot, full):
        gv, qk = full[:, 0:128], full[:, 128:256]
        gvb = gv.astype(BF16)
        gate_own[origin, 0:HR] = gvb[0:HR]
        gate_send[origin, 0:HR] = gvb[HR : 2 * HR]
        at_own = pl.multiple_of(core * HR, HR)
        at_sib = pl.multiple_of((1 - core) * HR, HR)
        pay[slot, pl.ds(at_own, HR)] = qk[0:HR].astype(BF16)
        pay[slot, pl.ds(at_sib, HR)] = qk[HR : 2 * HR].astype(BF16)
        low = low_lanes(HR)
        own_v, sib_v = gv[0:HR], gv[HR : 2 * HR]
        v_pair = jnp.where(
            is_first, jnp.where(low, swap(own_v), sib_v), jnp.where(low, swap(sib_v), own_v)
        )
        pay[slot, PAY_V : PAY_V + HR] = v_pair.astype(BF16)
        first = iota((16, 128), 0) == core
        pay[slot, PAY_B : PAY_B + 16] = jnp.where(
            first, bucket_own[...].astype(F32), bucket_sib[...].astype(F32)
        ).astype(BF16)

    def pack_cand(origin, slot, full):
        gvb, qk = full[:, 0:128].astype(BF16), full[:, 128:256]
        gate_own[origin, HR : HR + CR] = gvb[0:CR]
        gate_send[origin, HR : HR + CR] = gvb[CR : 2 * CR]
        own_q, sib_q = qk[0:CR], qk[CR : 2 * CR]
        q_pair = jnp.where(is_first, join(own_q, sib_q), join(sib_q, own_q))
        pay[slot, PAY_Q : PAY_Q + CR] = q_pair.astype(BF16)

    def pay_copy(rel):
        to = (y + rel + NY // 2) % NY
        return remote(pay.at[rel], got.at[y], pay_s.at[rel], pay_r.at[rel], (user, to * 2 + core))

    def first_copy(at, rows, sem):
        to = (y + NY // 2) % NY
        return remote(
            pay.at[0, pl.ds(at, rows)],
            got.at[y, pl.ds(at, rows)],
            pay_s.at[sem],
            pay_r.at[sem],
            (user, to * 2 + core),
        )

    first_hist = first_copy(0, PAY_Q, 0)
    first_cand = first_copy(PAY_Q, CR, 4)

    def project_step(step):
        project(((y + step) % NY, step), ((y + NY - step) % NY, NY - step))
        pay_copy(step).start()
        pay_copy(NY - step).start()

    own_feats.wait()
    own_weight.wait()
    remote(hist_in, feats.at[pl.ds(HR, HR)], sib_s.at[0], sib_r.at[0], sibling).wait_recv()
    remote(bucket_own, bucket_sib, sib_s.at[1], sib_r.at[1], sibling).wait_recv()
    pack_hist(y, 0, half_silu(dot(feats[0 : 2 * HR], weights[y]) * 0.5))
    first_hist.start()
    ring_step(1)
    ring_step(2)

    def cand_wait(t, carry):
        cand_copy(t).wait_recv()
        return carry

    lax.fori_loop(1, NU, cand_wait, 0)
    own_cand.wait()
    for k, columns in enumerate(join_rows(cand_arr)):
        feats[2 * HR : 2 * HR + CR, 128 * k : 128 * k + 128] = columns
    go(
        remote(
            feats.at[pl.ds(2 * HR, CR)],
            feats.at[pl.ds(2 * HR + CR, CR)],
            sib_s.at[2],
            sib_r.at[2],
            sibling,
        )
    )
    remote(
        feats.at[pl.ds(2 * HR, CR)],
        feats.at[pl.ds(2 * HR + CR, CR)],
        sib_s.at[2],
        sib_r.at[2],
        sibling,
    ).wait_recv()
    pack_cand(y, 0, half_silu(dot(feats[2 * HR :], weights[y]) * 0.5))
    first_cand.start()
    head_sel = iota((16, 128), 0) == 2 * ((y + NY // 2) % NY) + core
    table = jnp.concatenate([bias_in[...], jnp.zeros((16, 96), F32)], axis=1) * 0.5
    bias_row = jnp.sum(jnp.where(head_sel, table, 0.0), axis=0, keepdims=True)
    bias_hi = bias_row.astype(BF16).astype(F32)
    bias_lo = bias_row - bias_hi
    bias_lanes = pltpu.roll(jnp.broadcast_to(bias_hi, (8, 128)), DH, axis=1) + pltpu.roll(
        jnp.broadcast_to(bias_lo, (8, 128)), DH + NB, axis=1
    )
    bias_lanes = bias_lanes[0:1]
    length = length_in[0]

    low = low_lanes(HR)
    lane_h = iota((HR, 128), 1)
    row_h = iota((HR, 128), 0)

    def prepare(src):
        v_pair = got[src, PAY_V : PAY_V + HR].astype(F32)
        v_swap = swap(v_pair)
        buckets = got[src, PAY_B : PAY_B + 16].astype(F32)
        base = src * (2 * HR)
        for c in range(2):
            qk = got[src, c * HR : c * HR + HR].astype(F32)
            at = c * HR
            queries[src, at : at + HR] = jnp.where(low, qk * 0.0625, bias_lanes).astype(BF16)
            mine_b = jnp.sum(jnp.where(lane_h == row_h, buckets[c : c + 1], 0.0), axis=1, keepdims=True)
            hit = jnp.where((lane_h & (NB - 1)).astype(F32) == mine_b, 1.0, 0.0)
            keys[src, at : at + HR] = jnp.where(low, swap(qk), hit).astype(BF16)
            v = jnp.where(low, v_pair, v_swap) if c == 0 else jnp.where(low, v_swap, v_pair)
            values[src, at : at + HR] = jnp.where(row_h + (base + at) < length, v, 0.0).astype(BF16)
        q_pair = got[src, PAY_Q : PAY_Q + CR].astype(F32)
        low_c = low_lanes(CR)
        at = 2 * HR
        queries[src, at : at + CR] = jnp.where(low_c, q_pair * 0.0625, bias_lanes).astype(BF16)
        queries[src, at + CR : at + 2 * CR] = jnp.where(low_c, swap(q_pair) * 0.0625, bias_lanes).astype(BF16)

    def source(m):
        return (y + NY // 2 + jnp.where(m % 2 == 1, (m + 1) // 2, NY - m // 2)) % NY

    def weigh(q, src, mask=None):
        w = half_silu(dot_nt(q, keys[src]))
        if mask is not None:
            w = jnp.where(mask, w, 0.0)
        return dot(w.astype(BF16), values[src])

    def take_in(*new):
        for m in new:
            prepare(source(m))
        tri = iota((2 * HR + 2 * CR, 2 * HR), 1) <= iota((2 * HR + 2 * CR, 2 * HR), 0)
        own = [source(m) for m in new]
        for n, part_sum in [(n, weigh(queries[n], n, tri)) for n in own]:
            acc[n] = part_sum
        pairs = [(source(m), source(k)) for m in new for k in range(m)]
        for at in range(0, len(pairs), 4):
            sums = []
            for n, a in pairs[at : at + 4]:
                later, earlier = jnp.where(a < n, n, a), jnp.where(a < n, a, n)
                sums.append((later, 0, weigh(queries[later], earlier)))
                sums.append((earlier, 2 * HR, weigh(queries[earlier, 2 * HR :], later)))
            for src, first, part_sum in sums:
                acc[src, first:] += part_sum

    def take_in_step(step):
        pay_copy(NY - step).wait_recv()
        pay_copy(step).wait_recv()
        take_in(2 * step - 1, 2 * step)

    def back_c_copy(to):
        return remote(
            back_c.at[to], arr_c.at[seq], back_cs.at[to], back_cr.at[seq], (user, to)
        )

    def back_h_copy(to):
        return remote(
            back_h.at[to], arr_h.at[seq], back_hs.at[to], back_hr.at[seq], (user, to)
        )

    def send_back(to, copy, out, arr):
        @pl.when(to != seq)
        def _():
            copy(to).start()

        @pl.when(to == seq)
        def _():
            arr[seq] = out

    def send_cands():
        for off in (4, 3, 5, 2, 6, 1, 7, 0):
            i = (y + off) % NY
            for c in range(2):
                at = 2 * HR + c * CR
                lo, hi = acc[i, at : at + CR // 2], acc[i, at + CR // 2 : at + CR]
                packed = jnp.where(low_lanes(CR // 2), lo, hi).astype(BF16)
                to = i * 2 + c
                back_c[to] = packed
                if off:
                    back_c_copy(to).start()
                else:
                    send_back(to, back_c_copy, packed, arr_c)

    def send_hist(i, carry):
        for c in range(2):
            at = c * HR
            lo, hi = acc[i, at : at + HR // 2], acc[i, at + HR // 2 : at + HR]
            packed = jnp.where(low_lanes(HR // 2), lo, hi).astype(BF16)
            to = i * 2 + c
            back_h[to] = packed
            send_back(to, back_h_copy, packed, arr_h)
        return carry

    side_step(1)
    project_step(1)
    ring_step(3)
    side_step(2)
    project_step(2)
    ring_step(4)
    side_step(3)
    project_step(3)
    first_hist.wait_recv()
    first_cand.wait_recv()
    take_in(0)
    take_in_step(1)
    side_step(4)
    project(((y + 4) % NY, 4))
    own_pay = pltpu.make_async_copy(pay.at[4], got.at[y], local_sem.at[4])
    own_pay.start()
    gate_copy = remote(gate_send, gate_sib, sib_s.at[3], sib_r.at[3], sibling)
    go(gate_copy)
    take_in_step(2)
    take_in_step(3)
    last = source(7)
    lax.fori_loop(0, last, send_hist, 0)
    own_pay.wait()
    take_in(7)
    send_cands()
    lax.fori_loop(last, NY, send_hist, 0)

    def wait_back(copy_sem, arr, back):
        def one(t, carry):
            src = (seq + t) % NS
            remote(back.at[src], arr.at[src], copy_sem[0].at[src], copy_sem[1].at[src], (user, src)).wait_recv()
            return carry

        lax.fori_loop(1, NS, one, 0)

    def finish(arr, rows, at, inputs):
        half = rows // 2
        low_half = low_lanes(half)
        tiles, total = [], jnp.zeros((rows, 128), F32)
        for p in range(NY):
            at_p = 2 * ((p + NY // 2) % NY)
            even, odd = arr[at_p].astype(F32), arr[at_p + 1].astype(F32)
            tile = jnp.concatenate(
                [jnp.where(low_half, even, swap(odd)), jnp.where(low_half, swap(even), odd)], axis=0
            )
            tiles.append(tile)
            total = total + tile
        mean = jnp.sum(total, axis=1, keepdims=True) * (1.0 / D)
        tiles = [t - mean for t in tiles]
        squares = jnp.zeros((rows, 128), F32)
        for t in tiles:
            squares = squares + t * t
        var = jnp.sum(squares, axis=1, keepdims=True) * (1.0 / D)
        scale = lax.rsqrt(var + NORM_EPS)
        gated = [
            (t * scale * gain_gate[at : at + rows, 128 * p : 128 * p + 128]).astype(BF16)
            for p, t in enumerate(tiles)
        ]
        result = dot(jnp.concatenate(gated, axis=1), out_w[...])
        return result + inputs.astype(F32)

    gate_copy.wait_recv()
    own_out_w.wait()
    for p in range(NY):
        own, sib = gate_own[p].astype(F32), gate_sib[p].astype(F32)
        even, odd = jnp.where(is_first, own, sib), jnp.where(is_first, sib, own)
        columns = slice(128 * p, 128 * p + 128)
        gain_gate[:, columns] = join(even, odd) * gain_in[:, columns]
    wait_back((back_cs, back_cr), arr_c, back_c)
    cand_done = finish(arr_c, CR, HR, feats[2 * HR : 2 * HR + CR])
    split_rows(cand_done, done_send)

    def done_copy(t):
        to = (user + t) % NU
        return remote(
            done_send.at[pl.ds(pl.multiple_of(to * 16, 16), 16)],
            done_arr.at[pl.ds(pl.multiple_of(user * 16, 16), 16)],
            done_s.at[t],
            done_r.at[t],
            (to, seq),
        )

    def done_start(t, carry):
        done_copy(t).start()
        return carry

    lax.fori_loop(1, NU, done_start, 0)
    own_done = pltpu.make_async_copy(done_send.at[mine], done_arr.at[mine], local_sem.at[5])
    own_done.start()

    wait_back((back_hs, back_hr), arr_h, back_h)
    hist_out[...] = finish(arr_h, HR, 0, feats[0:HR]).astype(BF16)

    def done_wait(t, carry):
        done_copy(t).wait_recv()
        return carry

    lax.fori_loop(1, NU, done_wait, 0)
    own_done.wait()
    pick = jnp.where(iota((32, CR), 1).astype(F32) == slot_col, 1.0, 0.0).astype(BF16)
    for k, columns in enumerate(join_rows(done_arr)):
        cand_out[:, 128 * k : 128 * k + 128] = dot(pick, columns).astype(BF16)

    for copy in sent:
        copy.wait_send()

    def user_sends(t, carry):
        cand_copy(t).wait_send()
        done_copy(t).wait_send()
        return carry

    def pay_sends(t, carry):
        pay_copy(t).wait_send()
        pay_copy(NY - t).wait_send()
        return carry

    first_hist.wait_send()
    first_cand.wait_send()

    def back_sends(t, carry):
        to = (seq + t) % NS
        back_c_copy(to).wait_send()
        back_h_copy(to).wait_send()
        return carry

    lax.fori_loop(1, NU, user_sends, 0)
    lax.fori_loop(1, NY // 2, pay_sends, 0)
    lax.fori_loop(1, NS, back_sends, 0)


def body(hist, length, bucket, cand, owner, weight, bias, gain, out_weight):
    vmem = pl.BlockSpec(memory_space=pltpu.VMEM)
    hbm = pl.BlockSpec(memory_space=pltpu.HBM)
    dma = pltpu.SemaphoreType.DMA
    hist_out, cand_out = pl.pallas_call(
        kernel,
        out_shape=(
            jax.ShapeDtypeStruct((HR, D), BF16),
            jax.ShapeDtypeStruct((32, D), BF16),
        ),
        in_specs=[hbm] * 9,
        out_specs=(vmem, vmem),
        scratch_shapes=[
            pltpu.VMEM((HR, D), BF16),
            pltpu.VMEM((HR + CR, D), F32),
            pltpu.SMEM((1,), jnp.int32),
            pltpu.VMEM((1, 128), jnp.int32),
            pltpu.VMEM((32, D), BF16),
            pltpu.VMEM((1, 32), jnp.int32),
            pltpu.VMEM((NS, NB), F32),
            pltpu.VMEM((1, D), F32),
            pltpu.VMEM((2 * HR + 2 * CR, D), BF16),
            pltpu.VMEM((NY, D, 4 * DH), BF16),
            pltpu.VMEM((D, D), BF16),
            pltpu.VMEM((16, 128), BF16),
            pltpu.VMEM((16, 128), BF16),
            pltpu.VMEM((512, 128), BF16),
            pltpu.VMEM((512, 128), BF16),
            pltpu.VMEM((NY, PAY, 128), BF16),
            pltpu.VMEM((NY, PAY, 128), BF16),
            pltpu.VMEM((NY, HR + CR, 128), BF16),
            pltpu.VMEM((NY, HR + CR, 128), BF16),
            pltpu.VMEM((NY, HR + CR, 128), BF16),
            pltpu.VMEM((512, 128), F32),
            pltpu.VMEM((NY, 2 * HR + 2 * CR, 128), BF16),
            pltpu.VMEM((NY, 2 * HR, 128), BF16),
            pltpu.VMEM((NY, 2 * HR, 128), BF16),
            pltpu.VMEM((NY, 2 * HR + 2 * CR, 128), F32),
            pltpu.VMEM((NS, CR // 2, 128), BF16),
            pltpu.VMEM((NS, HR // 2, 128), BF16),
            pltpu.VMEM((NS, CR // 2, 128), BF16),
            pltpu.VMEM((NS, HR // 2, 128), BF16),
            pltpu.VMEM((512, 128), BF16),
            pltpu.VMEM((512, 128), BF16),
            dma((13,)),
            dma((2, 4, 4)),
            dma((2, 4, 4)),
            dma((7, 2, 2)),
            dma((7, 2, 2)),
            dma((7, 2)),
            dma((7, 2)),
            dma((NU,)),
            dma((NU,)),
            dma((NY,)),
            dma((NY,)),
            dma((4,)),
            dma((4,)),
            dma((NS,)),
            dma((NS,)),
            dma((NS,)),
            dma((NS,)),
            dma((NU,)),
            dma((NU,)),
        ],
        compiler_params=pltpu.CompilerParams(
            collective_id=0, has_side_effects=True, vmem_limit_bytes=48 * 1024 * 1024
        ),
        cost_estimate=pl.CostEstimate(
            flops=4 * 10**9, bytes_accessed=8 * 10**6, transcendentals=5 * 10**6
        ),
    )(
        *[
            a if a is length else pltpu.with_memory_space_constraint(a, pltpu.HBM)
            for a in (
                hist.reshape(HR, D),
                length,
                bucket,
                cand,
                owner.reshape(1, 32),
                weight.reshape(D, 4 * DH),
                bias,
                gain.reshape(1, D),
                out_weight,
            )
        ]
    )
    return hist_out.reshape(1, HR, D), cand_out


def solution(mesh):
    in_specs = (
        P("user", "seq", None),
        P("user"),
        P("user", "seq"),
        P(("user", "seq"), None),
        P(("user", "seq"), None),
        P(None, "seq", None),
        P(),
        P(),
        P(),
    )
    out_specs = (P("user", "seq", None), P(("user", "seq"), None))
    return jax.shard_map(body, mesh=mesh, in_specs=in_specs, out_specs=out_specs, check_vma=False)
```

```python
import functools

import jax
import jax.numpy as jnp
from jax import lax
from jax.experimental import pallas as pl
from jax.experimental.pallas import tpu as pltpu
from jax.sharding import PartitionSpec as P

MESH = pl.DeviceIdType.MESH
NORM_EPS = 1e-05
NX, NZ, NY = 4, 8, 8
NU, NS = NX * NZ, NY * 2
D = 1024
DH = 64
NB = 32
HR = 128
CR = 64
HIST = HR * NS
PAY_V = 2 * HR
PAY_B = 3 * HR
PAY_Q = PAY_B + 16
PAY = PAY_Q + CR
F32 = jnp.float32
BF16 = jnp.bfloat16


def dot(a, b):
    return jnp.dot(a, b, preferred_element_type=F32)


def dot_nt(a, b):
    return lax.dot_general(a, b, (((1,), (1,)), ((), ())), preferred_element_type=F32)


def iota(shape, axis):
    return lax.broadcasted_iota(jnp.int32, shape, axis)


def half_silu(h):
    return h * jnp.tanh(h) + h


def swap(a):
    return pltpu.roll(a, DH, axis=1)


def low_lanes(rows):
    return iota((rows, 128), 1) < DH


def join(lo, hi):
    return jnp.where(low_lanes(lo.shape[0]), lo, swap(hi))


def kernel(
    hist_in,
    length_hbm,
    bucket_hbm,
    cand_hbm,
    owner_hbm,
    weight_in,
    bias_hbm,
    gain_hbm,
    out_w_in,
    hist_out,
    cand_out,
    hist_done,
    gain_gate,
    length_in,
    bucket_in,
    cand_in,
    owner_in,
    bias_in,
    gain_in,
    feats,
    weights,
    out_w,
    bucket_own,
    bucket_sib,
    cand_send,
    cand_arr,
    pay,
    got,
    gate_own,
    gate_send,
    gate_sib,
    wide,
    queries,
    keys,
    values,
    acc,
    back_c,
    back_h,
    arr_c,
    arr_h,
    done_send,
    done_arr,
    local_sem,
    ring_s,
    ring_r,
    side_s,
    side_r,
    far_s,
    far_r,
    cand_s,
    cand_r,
    pay_s,
    pay_r,
    sib_s,
    sib_r,
    back_cs,
    back_cr,
    back_hs,
    back_hr,
    done_s,
    done_r,
):
    user = lax.axis_index("user")
    seq = lax.axis_index("seq")
    x, z = user // NZ, user % NZ
    y, core = seq // 2, seq % 2
    part = (x + z) % 4
    sibling = (user, y * 2 + (1 - core))

    def along_y(step):
        return (user, ((y + NY + step) % NY) * 2 + core)

    def along_x(step):
        return (((x + NX + step) % NX) * NZ + z, seq)

    def along_z(step):
        return (x * NZ + (z + NZ + step) % NZ, seq)

    def remote(src, dst, send, recv, to):
        return pltpu.make_async_remote_copy(
            src_ref=src, dst_ref=dst, send_sem=send, recv_sem=recv, device_id=to, device_id_type=MESH
        )

    barrier = pltpu.get_barrier_semaphore()

    def greet_user(t, carry):
        pl.semaphore_signal(barrier, inc=1, device_id=((user + t) % NU, seq), device_id_type=MESH)
        return carry

    def greet_seq(t, carry):
        pl.semaphore_signal(barrier, inc=1, device_id=(user, (seq + t) % NS), device_id_type=MESH)
        return carry

    lax.fori_loop(1, NU, greet_user, 0)
    lax.fori_loop(1, NS, greet_seq, 0)

    own_weight = pltpu.make_async_copy(weight_in, weights.at[y], local_sem.at[0])
    own_feats = pltpu.make_async_copy(hist_in, feats.at[pl.ds(0, HR)], local_sem.at[1])
    own_out_w = pltpu.make_async_copy(out_w_in, out_w, local_sem.at[2])
    small = [
        pltpu.make_async_copy(src, dst, local_sem.at[6 + n])
        for n, (src, dst) in enumerate(
            (
                (owner_hbm, owner_in),
                (cand_hbm, cand_in),
                (bucket_hbm, bucket_in),
                (length_hbm, length_in),
                (bias_hbm, bias_in),
                (gain_hbm, gain_in),
            )
        )
    ]
    for copy in small:
        copy.start()
    own_weight.start()
    own_feats.start()
    own_out_w.start()

    for copy in small:
        copy.wait()
    lane = iota((32, 128), 1)
    row = iota((32, 128), 0)
    owner_row = jnp.concatenate([owner_in[...].astype(F32), jnp.zeros((1, 96), F32)], axis=1)
    owner_wide = jnp.broadcast_to(owner_row, (32, 128))
    owner_col = jnp.sum(jnp.where(lane == row, owner_wide, 0.0), axis=1, keepdims=True)
    same = (owner_wide == owner_col) & (lane < 32)
    rank_row = jnp.sum(jnp.where(same & (row < lane), 1.0, 0.0), axis=0, keepdims=True)
    rank_col = jnp.sum(jnp.where(same & (lane < row), 1.0, 0.0), axis=1, keepdims=True)
    slot_row = owner_row * 2.0 + rank_row
    slot_col = owner_col * 2.0 + rank_col

    def split_rows(slots, out):
        for k in range(8):
            wide[pl.ds(k, CR, stride=8), :] = slots[:, 128 * k : 128 * k + 128]
        out[...] = wide[...].astype(BF16)

    def join_rows(arrived):
        wide[...] = arrived[...].astype(F32)
        return [wide[pl.ds(k, CR, stride=8), :].astype(BF16) for k in range(8)]

    put = jnp.where(iota((CR, 32), 0).astype(F32) == slot_row[:, 0:32], 1.0, 0.0).astype(BF16)
    split_rows(dot(put, cand_in[...]), cand_send)
    bucket_own[...] = jnp.broadcast_to(bucket_in[...].astype(F32), (16, 128)).astype(BF16)

    pl.semaphore_wait(barrier, NU - 1 + NS - 1)

    sent = []

    def go(copy):
        copy.start()
        sent.append(copy)

    def quarter(origin, cls, half, at=0, rows=128):
        start = pl.multiple_of(cls * 256 + half * 128 + at, 64)
        return weights.at[origin, pl.ds(start, rows)]

    def ring_copy(dirn, step, piece, src):
        sign = 1 if dirn == 0 else -1
        origin = (y + NY - sign * (step - 1)) % NY
        dst = quarter(origin, part, piece // 2, 64 * (piece % 2), 64)
        return remote(
            dst if src is None else src,
            dst,
            ring_s.at[dirn, step - 1, piece],
            ring_r.at[dirn, step - 1, piece],
            along_y(sign),
        )

    for piece in range(4):
        start = pl.multiple_of(part * 256 + piece * 64, 64)
        for dirn in range(2):
            go(ring_copy(dirn, 1, piece, weight_in.at[pl.ds(start, 64)]))
    go(remote(hist_in, feats.at[pl.ds(HR, HR)], sib_s.at[0], sib_r.at[0], sibling))

    go(remote(bucket_own, bucket_sib, sib_s.at[1], sib_r.at[1], sibling))

    def cand_copy(t):
        to = (user + t) % NU
        return remote(
            cand_send.at[pl.ds(pl.multiple_of(to * 16, 16), 16)],
            cand_arr.at[pl.ds(pl.multiple_of(user * 16, 16), 16)],
            cand_s.at[t],
            cand_r.at[t],
            (to, seq),
        )

    def cand_start(t, carry):
        cand_copy(t).start()
        return carry

    lax.fori_loop(1, NU, cand_start, 0)
    mine = pl.ds(pl.multiple_of(user * 16, 16), 16)
    own_cand = pltpu.make_async_copy(cand_send.at[mine], cand_arr.at[mine], local_sem.at[3])
    own_cand.start()

    def origin_of(dirn, step):
        sign = 1 if dirn == 0 else -1
        return (y + NY - sign * step) % NY

    def index_of(dirn, step):
        return 2 * (step - 1) + (dirn if step < 4 else 0)

    def side_copy(dirn, step, half, way):
        ref = quarter(origin_of(dirn, step), part, half)
        o = index_of(dirn, step)
        to = along_x(1 if way == 0 else -1)
        return remote(ref, ref, side_s.at[o, half, way], side_r.at[o, half, way], to)

    def far_copy(dirn, step, half):
        ref = quarter(origin_of(dirn, step), part, half)
        o = index_of(dirn, step)
        to = along_z(2 if half == 0 else -2)
        return remote(ref, ref, far_s.at[o, half], far_r.at[o, half], to)

    def ring_step(step):
        for half in range(2):
            for dirn in range(2):
                if step == 4 and dirn != half:
                    continue
                for piece in (2 * half, 2 * half + 1):
                    ring_copy(dirn, step, piece, None).wait_recv()
                    if step < 3 or (step == 3 and dirn == half):
                        go(ring_copy(dirn, step + 1, piece, None))
                for way in range(2):
                    go(side_copy(dirn, step, half, way))
                go(far_copy(dirn, step, half))

    def side_step(step):
        for half in range(2):
            for dirn in range(2 if step < 4 else 1):
                for way in range(2):
                    side_copy(dirn, step, half, way).wait_recv()
                far_copy(dirn, step, half).wait_recv()

    is_first = core == 0

    def project(*heads):
        sums = [dot(feats[...], weights[origin]) for origin, slot in heads]
        for (origin, slot), part_sum in zip(heads, sums):
            full = half_silu(part_sum * 0.5)
            pack_hist(origin, slot, full[0 : 2 * HR])
            pack_cand(origin, slot, full[2 * HR :])

    def pack_hist(origin, slot, full):
        gv, qk = full[:, 0:128], full[:, 128:256]
        gvb = gv.astype(BF16)
        gate_own[origin, 0:HR] = gvb[0:HR]
        gate_send[origin, 0:HR] = gvb[HR : 2 * HR]
        at_own = pl.multiple_of(core * HR, HR)
        at_sib = pl.multiple_of((1 - core) * HR, HR)
        pay[slot, pl.ds(at_own, HR)] = qk[0:HR].astype(BF16)
        pay[slot, pl.ds(at_sib, HR)] = qk[HR : 2 * HR].astype(BF16)
        low = low_lanes(HR)
        own_v, sib_v = gv[0:HR], gv[HR : 2 * HR]
        v_pair = jnp.where(
            is_first, jnp.where(low, swap(own_v), sib_v), jnp.where(low, swap(sib_v), own_v)
        )
        pay[slot, PAY_V : PAY_V + HR] = v_pair.astype(BF16)
        first = iota((16, 128), 0) == core
        pay[slot, PAY_B : PAY_B + 16] = jnp.where(
            first, bucket_own[...].astype(F32), bucket_sib[...].astype(F32)
        ).astype(BF16)

    def pack_cand(origin, slot, full):
        gvb, qk = full[:, 0:128].astype(BF16), full[:, 128:256]
        gate_own[origin, HR : HR + CR] = gvb[0:CR]
        gate_send[origin, HR : HR + CR] = gvb[CR : 2 * CR]
        own_q, sib_q = qk[0:CR], qk[CR : 2 * CR]
        q_pair = jnp.where(is_first, join(own_q, sib_q), join(sib_q, own_q))
        pay[slot, PAY_Q : PAY_Q + CR] = q_pair.astype(BF16)

    def pay_copy(rel):
        to = (y + rel + NY // 2) % NY
        return remote(pay.at[rel], got.at[y], pay_s.at[rel], pay_r.at[rel], (user, to * 2 + core))

    def first_copy(at, rows, sem):
        to = (y + NY // 2) % NY
        return remote(
            pay.at[0, pl.ds(at, rows)],
            got.at[y, pl.ds(at, rows)],
            pay_s.at[sem],
            pay_r.at[sem],
            (user, to * 2 + core),
        )

    first_hist = first_copy(0, PAY_Q, 0)
    first_cand = first_copy(PAY_Q, CR, 4)

    def project_step(step):
        project(((y + step) % NY, step), ((y + NY - step) % NY, NY - step))
        pay_copy(step).start()
        pay_copy(NY - step).start()

    own_feats.wait()
    own_weight.wait()
    remote(hist_in, feats.at[pl.ds(HR, HR)], sib_s.at[0], sib_r.at[0], sibling).wait_recv()
    remote(bucket_own, bucket_sib, sib_s.at[1], sib_r.at[1], sibling).wait_recv()
    pack_hist(y, 0, half_silu(dot(feats[0 : 2 * HR], weights[y]) * 0.5))
    first_hist.start()
    ring_step(1)
    ring_step(2)

    def cand_wait(t, carry):
        cand_copy(t).wait_recv()
        return carry

    lax.fori_loop(1, NU, cand_wait, 0)
    own_cand.wait()
    for k, columns in enumerate(join_rows(cand_arr)):
        feats[2 * HR : 2 * HR + CR, 128 * k : 128 * k + 128] = columns
    go(
        remote(
            feats.at[pl.ds(2 * HR, CR)],
            feats.at[pl.ds(2 * HR + CR, CR)],
            sib_s.at[2],
            sib_r.at[2],
            sibling,
        )
    )
    remote(
        feats.at[pl.ds(2 * HR, CR)],
        feats.at[pl.ds(2 * HR + CR, CR)],
        sib_s.at[2],
        sib_r.at[2],
        sibling,
    ).wait_recv()
    pack_cand(y, 0, half_silu(dot(feats[2 * HR :], weights[y]) * 0.5))
    first_cand.start()
    head_sel = iota((16, 128), 0) == 2 * ((y + NY // 2) % NY) + core
    table = jnp.concatenate([bias_in[...], jnp.zeros((16, 96), F32)], axis=1) * 0.5
    bias_row = jnp.sum(jnp.where(head_sel, table, 0.0), axis=0, keepdims=True)
    bias_hi = bias_row.astype(BF16).astype(F32)
    bias_lo = bias_row - bias_hi
    bias_lanes = pltpu.roll(jnp.broadcast_to(bias_hi, (8, 128)), DH, axis=1) + pltpu.roll(
        jnp.broadcast_to(bias_lo, (8, 128)), DH + NB, axis=1
    )
    bias_lanes = bias_lanes[0:1]
    length = length_in[0]

    low = low_lanes(HR)
    lane_h = iota((HR, 128), 1)
    row_h = iota((HR, 128), 0)

    def prepare(src):
        v_pair = got[src, PAY_V : PAY_V + HR].astype(F32)
        v_swap = swap(v_pair)
        buckets = got[src, PAY_B : PAY_B + 16].astype(F32)
        base = src * (2 * HR)
        for c in range(2):
            qk = got[src, c * HR : c * HR + HR].astype(F32)
            at = c * HR
            queries[src, at : at + HR] = jnp.where(low, qk * 0.0625, bias_lanes).astype(BF16)
            mine_b = jnp.sum(jnp.where(lane_h == row_h, buckets[c : c + 1], 0.0), axis=1, keepdims=True)
            hit = jnp.where((lane_h & (NB - 1)).astype(F32) == mine_b, 1.0, 0.0)
            keys[src, at : at + HR] = jnp.where(low, swap(qk), hit).astype(BF16)
            v = jnp.where(low, v_pair, v_swap) if c == 0 else jnp.where(low, v_swap, v_pair)
            values[src, at : at + HR] = jnp.where(row_h + (base + at) < length, v, 0.0).astype(BF16)
        q_pair = got[src, PAY_Q : PAY_Q + CR].astype(F32)
        low_c = low_lanes(CR)
        at = 2 * HR
        queries[src, at : at + CR] = jnp.where(low_c, q_pair * 0.0625, bias_lanes).astype(BF16)
        queries[src, at + CR : at + 2 * CR] = jnp.where(low_c, swap(q_pair) * 0.0625, bias_lanes).astype(BF16)

    def source(m):
        return (y + NY // 2 + (0, 1, 7, 2, 6, 4, 3, 5)[m]) % NY

    def weigh(q, src, mask=None):
        w = half_silu(dot_nt(q, keys[src]))
        if mask is not None:
            w = jnp.where(mask, w, 0.0)
        return dot(w.astype(BF16), values[src])

    def take_in(*new):
        for m in new:
            prepare(source(m))
        tri = iota((2 * HR + 2 * CR, 2 * HR), 1) <= iota((2 * HR + 2 * CR, 2 * HR), 0)
        own = [source(m) for m in new]
        for n, part_sum in [(n, weigh(queries[n], n, tri)) for n in own]:
            acc[n] = part_sum
        pairs = [(source(m), source(k)) for m in new for k in range(m)]
        for at in range(0, len(pairs), 4):
            sums = []
            for n, a in pairs[at : at + 4]:
                later, earlier = jnp.where(a < n, n, a), jnp.where(a < n, a, n)
                sums.append((later, 0, weigh(queries[later], earlier)))
                sums.append((earlier, 2 * HR, weigh(queries[earlier, 2 * HR :], later)))
            for src, first, part_sum in sums:
                acc[src, first:] += part_sum

    def take_in_step(step):
        pay_copy(NY - step).wait_recv()
        pay_copy(step).wait_recv()
        if step < 3:
            take_in(2 * step - 1, 2 * step)
        else:
            take_in(6, 7)

    def back_c_copy(to):
        return remote(
            back_c.at[to], arr_c.at[seq], back_cs.at[to], back_cr.at[seq], (user, to)
        )

    def back_h_copy(to):
        return remote(
            back_h.at[to], arr_h.at[seq], back_hs.at[to], back_hr.at[seq], (user, to)
        )

    def send_back(to, copy, out, arr):
        @pl.when(to != seq)
        def _():
            copy(to).start()

        @pl.when(to == seq)
        def _():
            arr[seq] = out

    def send_cands():
        for off in (4, 3, 5, 2, 6, 1, 7, 0):
            i = (y + off) % NY
            for c in range(2):
                at = 2 * HR + c * CR
                lo, hi = acc[i, at : at + CR // 2], acc[i, at + CR // 2 : at + CR]
                packed = jnp.where(low_lanes(CR // 2), lo, hi).astype(BF16)
                to = i * 2 + c
                back_c[to] = packed
                if off:
                    back_c_copy(to).start()
                else:
                    send_back(to, back_c_copy, packed, arr_c)

    def send_hist(i, carry):
        for c in range(2):
            at = c * HR
            lo, hi = acc[i, at : at + HR // 2], acc[i, at + HR // 2 : at + HR]
            packed = jnp.where(low_lanes(HR // 2), lo, hi).astype(BF16)
            to = i * 2 + c
            back_h[to] = packed
            send_back(to, back_h_copy, packed, arr_h)
        return carry

    side_step(1)
    project_step(1)
    ring_step(3)
    side_step(2)
    project_step(2)
    ring_step(4)
    side_step(3)
    project_step(3)
    first_hist.wait_recv()
    first_cand.wait_recv()
    take_in(0)
    take_in_step(1)
    side_step(4)
    project(((y + 4) % NY, 4))
    own_pay = pltpu.make_async_copy(pay.at[4], got.at[y], local_sem.at[4])
    own_pay.start()
    gate_copy = remote(gate_send, gate_sib, sib_s.at[3], sib_r.at[3], sibling)
    go(gate_copy)
    take_in_step(2)
    own_pay.wait()
    take_in(5)
    last = jnp.where(source(6) < source(7), source(6), source(7))
    lax.fori_loop(0, last, send_hist, 0)
    take_in_step(3)
    send_cands()
    lax.fori_loop(last, NY, send_hist, 0)

    def wait_back(copy_sem, arr, back):
        def one(t, carry):
            src = (seq + t) % NS
            remote(back.at[src], arr.at[src], copy_sem[0].at[src], copy_sem[1].at[src], (user, src)).wait_recv()
            return carry

        lax.fori_loop(1, NS, one, 0)

    def finish(arr, rows, at, inputs):
        half = rows // 2
        low_half = low_lanes(half)
        tiles, total = [], jnp.zeros((rows, 128), F32)
        for p in range(NY):
            at_p = 2 * ((p + NY // 2) % NY)
            even, odd = arr[at_p].astype(F32), arr[at_p + 1].astype(F32)
            tile = jnp.concatenate(
                [jnp.where(low_half, even, swap(odd)), jnp.where(low_half, swap(even), odd)], axis=0
            )
            tiles.append(tile)
            total = total + tile
        mean = jnp.sum(total, axis=1, keepdims=True) * (1.0 / D)
        tiles = [t - mean for t in tiles]
        squares = jnp.zeros((rows, 128), F32)
        for t in tiles:
            squares = squares + t * t
        var = jnp.sum(squares, axis=1, keepdims=True) * (1.0 / D)
        scale = lax.rsqrt(var + NORM_EPS)
        gated = [
            (t * scale * gain_gate[at : at + rows, 128 * p : 128 * p + 128]).astype(BF16)
            for p, t in enumerate(tiles)
        ]
        result = dot(jnp.concatenate(gated, axis=1), out_w[...])
        return result + inputs.astype(F32)

    gate_copy.wait_recv()
    own_out_w.wait()
    for p in range(NY):
        own, sib = gate_own[p].astype(F32), gate_sib[p].astype(F32)
        even, odd = jnp.where(is_first, own, sib), jnp.where(is_first, sib, own)
        columns = slice(128 * p, 128 * p + 128)
        gain_gate[:, columns] = join(even, odd) * gain_in[:, columns]
    wait_back((back_cs, back_cr), arr_c, back_c)
    cand_done = finish(arr_c, CR, HR, feats[2 * HR : 2 * HR + CR])
    split_rows(cand_done, done_send)

    def done_copy(t):
        to = (user + t) % NU
        return remote(
            done_send.at[pl.ds(pl.multiple_of(to * 16, 16), 16)],
            done_arr.at[pl.ds(pl.multiple_of(user * 16, 16), 16)],
            done_s.at[t],
            done_r.at[t],
            (to, seq),
        )

    def done_start(t, carry):
        done_copy(t).start()
        return carry

    lax.fori_loop(1, NU, done_start, 0)
    own_done = pltpu.make_async_copy(done_send.at[mine], done_arr.at[mine], local_sem.at[5])
    own_done.start()

    wait_back((back_hs, back_hr), arr_h, back_h)
    hist_out[...] = finish(arr_h, HR, 0, feats[0:HR]).astype(BF16)

    def done_wait(t, carry):
        done_copy(t).wait_recv()
        return carry

    lax.fori_loop(1, NU, done_wait, 0)
    own_done.wait()
    pick = jnp.where(iota((32, CR), 1).astype(F32) == slot_col, 1.0, 0.0).astype(BF16)
    for k, columns in enumerate(join_rows(done_arr)):
        cand_out[:, 128 * k : 128 * k + 128] = dot(pick, columns).astype(BF16)

    for copy in sent:
        copy.wait_send()

    def user_sends(t, carry):
        cand_copy(t).wait_send()
        done_copy(t).wait_send()
        return carry

    def pay_sends(t, carry):
        pay_copy(t).wait_send()
        pay_copy(NY - t).wait_send()
        return carry

    first_hist.wait_send()
    first_cand.wait_send()

    def back_sends(t, carry):
        to = (seq + t) % NS
        back_c_copy(to).wait_send()
        back_h_copy(to).wait_send()
        return carry

    lax.fori_loop(1, NU, user_sends, 0)
    lax.fori_loop(1, NY // 2, pay_sends, 0)
    lax.fori_loop(1, NS, back_sends, 0)


def body(hist, length, bucket, cand, owner, weight, bias, gain, out_weight):
    vmem = pl.BlockSpec(memory_space=pltpu.VMEM)
    hbm = pl.BlockSpec(memory_space=pltpu.HBM)
    dma = pltpu.SemaphoreType.DMA
    hist_out, cand_out = pl.pallas_call(
        kernel,
        out_shape=(
            jax.ShapeDtypeStruct((HR, D), BF16),
            jax.ShapeDtypeStruct((32, D), BF16),
        ),
        in_specs=[hbm] * 9,
        out_specs=(vmem, vmem),
        scratch_shapes=[
            pltpu.VMEM((HR, D), BF16),
            pltpu.VMEM((HR + CR, D), F32),
            pltpu.SMEM((1,), jnp.int32),
            pltpu.VMEM((1, 128), jnp.int32),
            pltpu.VMEM((32, D), BF16),
            pltpu.VMEM((1, 32), jnp.int32),
            pltpu.VMEM((NS, NB), F32),
            pltpu.VMEM((1, D), F32),
            pltpu.VMEM((2 * HR + 2 * CR, D), BF16),
            pltpu.VMEM((NY, D, 4 * DH), BF16),
            pltpu.VMEM((D, D), BF16),
            pltpu.VMEM((16, 128), BF16),
            pltpu.VMEM((16, 128), BF16),
            pltpu.VMEM((512, 128), BF16),
            pltpu.VMEM((512, 128), BF16),
            pltpu.VMEM((NY, PAY, 128), BF16),
            pltpu.VMEM((NY, PAY, 128), BF16),
            pltpu.VMEM((NY, HR + CR, 128), BF16),
            pltpu.VMEM((NY, HR + CR, 128), BF16),
            pltpu.VMEM((NY, HR + CR, 128), BF16),
            pltpu.VMEM((512, 128), F32),
            pltpu.VMEM((NY, 2 * HR + 2 * CR, 128), BF16),
            pltpu.VMEM((NY, 2 * HR, 128), BF16),
            pltpu.VMEM((NY, 2 * HR, 128), BF16),
            pltpu.VMEM((NY, 2 * HR + 2 * CR, 128), F32),
            pltpu.VMEM((NS, CR // 2, 128), BF16),
            pltpu.VMEM((NS, HR // 2, 128), BF16),
            pltpu.VMEM((NS, CR // 2, 128), BF16),
            pltpu.VMEM((NS, HR // 2, 128), BF16),
            pltpu.VMEM((512, 128), BF16),
            pltpu.VMEM((512, 128), BF16),
            dma((13,)),
            dma((2, 4, 4)),
            dma((2, 4, 4)),
            dma((7, 2, 2)),
            dma((7, 2, 2)),
            dma((7, 2)),
            dma((7, 2)),
            dma((NU,)),
            dma((NU,)),
            dma((NY,)),
            dma((NY,)),
            dma((4,)),
            dma((4,)),
            dma((NS,)),
            dma((NS,)),
            dma((NS,)),
            dma((NS,)),
            dma((NU,)),
            dma((NU,)),
        ],
        compiler_params=pltpu.CompilerParams(
            collective_id=0, has_side_effects=True, vmem_limit_bytes=48 * 1024 * 1024
        ),
        cost_estimate=pl.CostEstimate(
            flops=4 * 10**9, bytes_accessed=8 * 10**6, transcendentals=5 * 10**6
        ),
    )(
        *[
            a if a is length else pltpu.with_memory_space_constraint(a, pltpu.HBM)
            for a in (
                hist.reshape(HR, D),
                length,
                bucket,
                cand,
                owner.reshape(1, 32),
                weight.reshape(D, 4 * DH),
                bias,
                gain.reshape(1, D),
                out_weight,
            )
        ]
    )
    return hist_out.reshape(1, HR, D), cand_out


def solution(mesh):
    in_specs = (
        P("user", "seq", None),
        P("user"),
        P("user", "seq"),
        P(("user", "seq"), None),
        P(("user", "seq"), None),
        P(None, "seq", None),
        P(),
        P(),
        P(),
    )
    out_specs = (P("user", "seq", None), P(("user", "seq"), None))
    return jax.shard_map(body, mesh=mesh, in_specs=in_specs, out_specs=out_specs, check_vma=False)
```
